128 devices in a mesh: dp: 8 (over x_hi, y), slab: 16 (over z, x_lo, core).
Axes of the slice: x: 4 (x_hi: 2, x_lo: 2; x = x_hi * 2 + x_lo), y: 4, z: 4, core: 2. Of those that a mesh axis runs over, the one named last changes fastest.
Arguments:
- field: bfloat16 [8, 64, 64, 4096], P('dp', None, 'slab'), may hold values from -6 to 6
- cotangent: bfloat16 [8, 64, 64, 4096], P('dp', None, 'slab'), may hold values from -6 to 6
- spectral: bfloat16 [2, 64, 64, 32768], P(None, None, None, ('slab', 'dp')), may hold values from -1.5 to 1.5
- skip: bfloat16 [64, 64], replicated, may hold values from -0.75 to 0.75
- bias: float32 [64], replicated, may hold values from -3 to 3
Outputs:
- output: bfloat16 [8, 64, 64, 4096], P('dp', None, 'slab')
- field_grad: bfloat16 [8, 64, 64, 4096], P('dp', None, 'slab')
- spectral_grad: bfloat16 [2, 64, 64, 32768], P(None, None, None, ('slab', 'dp'))
- skip_grad: float32 [64, 64], replicated
- bias_grad: float32 [64], replicated
The draws below stay inside these ranges and needn't reach their ends.
All inputs are finite; a program needn't handle non-finite values.
Results may differ from the reference program's by a relative error of at most 0.015.
Values may be sent and summed in bfloat16 or wider, within the bound.
A program may use at most 192 MiB of HBM per device.

```python
import math
import jax
import jax.numpy as jnp
from jax import lax

C = 64
N = 64
M = 32
SAMPLES = 8


def steps_of(stream_key, extent, split, smallest, largest):
    def one(position, parts):
        draws = jax.random.uniform(jax.random.fold_in(jax.random.fold_in(stream_key, 6), position), (parts,), jnp.float32, smallest / len(split), largest / len(split))
        return jnp.repeat(jnp.exp(draws), extent[position] // parts).reshape((-1,) + (1,) * (len(extent) - position - 1))

    gain = one(*split[0])
    for cut in split[1:]:
        gain = gain * one(*cut)
    return gain


def noise(own_key, dims, deviation, limit, split=(), held_as=jnp.bfloat16):
    entries = jax.random.normal(own_key, dims, jnp.float32) * deviation
    if len(split) > 0:
        entries = steps_of(own_key, dims, split, -0.22, 0.18) * entries
    return jnp.clip(entries, min=-limit, max=limit).astype(held_as)


def setup_inputs(seed: int = 0) -> dict:
    arg_keys = jax.random.split(jax.random.key(seed), 6)
    return {
        "field": noise(arg_keys[0], (SAMPLES, C, N, N * N), 1.0, 6.0, ((0, 8), (2, 16))),
        "cotangent": noise(arg_keys[1], (SAMPLES, C, N, N * N), 1.0, 6.0, ((0, 8), (2, 16))),
        "spectral": noise(arg_keys[2], (2, C, C, M * M * M), (2 * C * M * M * M // (N * N * N)) ** -0.5, 1.5, ((3, 128),)),
        "skip": noise(arg_keys[3], (C, C), C ** -0.5, 0.75),
        "bias": noise(arg_keys[4], (C,), 0.5, 3.0, (), jnp.float32),
    }


def tables():
    places = jnp.arange(N, dtype=jnp.int32)
    frequency = jnp.arange(M, dtype=jnp.int32) - M // 2
    phases = jnp.mod(places[:, None] * frequency[None, :], N)
    angles = jnp.mod(phases[:, None, :, None] + phases[None, :, None, :], N).astype(jnp.float32) * (2.0 * math.pi / N)
    plane_table = (jnp.stack([jnp.cos(angles), -jnp.sin(angles)], axis=2) / N).reshape(N * N, 2, M * M)
    line_angle = phases.astype(jnp.float32) * (2.0 * math.pi / N)
    cosine = jnp.cos(line_angle) / math.sqrt(N)
    sine = jnp.sin(line_angle) / math.sqrt(N)
    line_table = jnp.stack([jnp.stack([cosine, -sine], 1), jnp.stack([sine, cosine], 1)], 0)
    return (plane_table.astype(jnp.bfloat16), line_table.astype(jnp.bfloat16))

def reference(field, cotangent, spectral, skip, bias):
    plane_table, line_table = tables()
    plane_wide = plane_table.astype(jnp.float32)
    line_wide = line_table.astype(jnp.float32)
    count = field.shape[0]

    def to_spectrum(values):
        planes = lax.map(lambda single: jnp.einsum('cxp,ptq->tcxq', single.astype(jnp.float32), plane_wide), values)
        planes = jnp.transpose(planes.astype(jnp.bfloat16), (1, 0, 2, 3, 4))
        modes = jnp.einsum('rbcxq,rxtk->tbcqk', planes.astype(jnp.float32), line_wide).astype(jnp.bfloat16)
        return modes.reshape(2, count, C, M * M * M)

    def to_spatial(modes):
        modes = modes.reshape(2, count, C, M * M, M).astype(jnp.float32)
        lines = jnp.einsum('rbcqk,txrk->tbcxq', modes, line_wide).astype(jnp.bfloat16)
        lines = jnp.transpose(lines, (1, 0, 2, 3, 4))
        return lax.map(lambda single: jnp.einsum('tcxq,ptq->cxp', single.astype(jnp.float32), plane_wide), lines)
    weight_re = spectral[0].astype(jnp.float32)
    weight_im = spectral[1].astype(jnp.float32)
    modes_in = to_spectrum(field)
    in_re = modes_in[0].astype(jnp.float32)
    in_im = modes_in[1].astype(jnp.float32)
    mixed_re = jnp.einsum('biq,ioq->boq', in_re, weight_re) - jnp.einsum('biq,ioq->boq', in_im, weight_im)
    mixed_im = jnp.einsum('biq,ioq->boq', in_re, weight_im) + jnp.einsum('biq,ioq->boq', in_im, weight_re)
    mixed = jnp.stack([mixed_re, mixed_im]).astype(jnp.bfloat16)
    spectral_part = to_spatial(mixed)
    skip_wide = skip.astype(jnp.float32)
    field_wide = field.astype(jnp.float32)
    pre = spectral_part + jnp.einsum('bixp,io->boxp', field_wide, skip_wide) + bias[None, :, None, None]
    activate = lambda values: jax.nn.gelu(values, approximate=True)
    pre_value, pullback = jax.vjp(activate, pre)
    output = pre_value.astype(jnp.bfloat16)
    pre_grad = pullback(cotangent.astype(jnp.float32))[0].astype(jnp.bfloat16)
    modes_grad = to_spectrum(pre_grad)
    grad_re = modes_grad[0].astype(jnp.float32)
    grad_im = modes_grad[1].astype(jnp.float32)
    back_re = jnp.einsum('boq,ioq->biq', grad_re, weight_re) + jnp.einsum('boq,ioq->biq', grad_im, weight_im)
    back_im = jnp.einsum('boq,ioq->biq', grad_im, weight_re) - jnp.einsum('boq,ioq->biq', grad_re, weight_im)
    back_modes = jnp.stack([back_re, back_im]).astype(jnp.bfloat16)
    spec_re = jnp.einsum('biq,boq->ioq', in_re, grad_re) + jnp.einsum('biq,boq->ioq', in_im, grad_im)
    spec_im = jnp.einsum('biq,boq->ioq', in_re, grad_im) - jnp.einsum('biq,boq->ioq', in_im, grad_re)
    spectral_grad = jnp.stack([spec_re, spec_im]).astype(jnp.bfloat16)
    pre_wide = pre_grad.astype(jnp.float32)
    field_grad = (to_spatial(back_modes) + jnp.einsum('boxp,io->bixp', pre_wide, skip_wide)).astype(jnp.bfloat16)
    factor = 1.0 / math.sqrt(SAMPLES * N * N * N)
    skip_grad = jnp.einsum('bixp,boxp->io', field_wide, pre_wide) * factor
    bias_grad = lax.optimization_barrier(jnp.sum(pre_wide, axis=(0, 2, 3))) * factor
    return (output, field_grad, spectral_grad, skip_grad, bias_grad)
```

```python
import functools
import math

import jax
import jax.numpy as jnp
import ml_dtypes
import numpy as np
from jax import lax
from jax.experimental import pallas as pl
from jax.experimental.pallas import tpu as pltpu
from jax.sharding import PartitionSpec as P

N = 64
M = 32
C = 64
DP = 8
SLAB = 16
DEVICES = DP * SLAB
SAMPLES = 8
BF = jnp.bfloat16
F32 = jnp.float32
MESH = pl.DeviceIdType.MESH
VMEM_LIMIT = 56 * 1024 * 1024


def waves():
    phase = np.mod(np.arange(N)[:, None] * (np.arange(M)[None, :] - M // 2), N)
    angle = phase * (2.0 * math.pi / N)
    return np.cos(angle) / 8.0, np.sin(angle) / 8.0


def tables():
    cos, sin = waves()
    pair = np.stack([cos, -sin], 0).reshape(2, N, 4, 8)
    d1 = np.einsum("tzbl,uv->butlvz", pair, np.eye(4)).reshape(256, 256)
    turn = np.stack([np.stack([cos, sin], 0), np.stack([-sin, cos], 0)], 0)
    turn = turn.reshape(2, 2, N, SLAB, 2)
    d2 = np.einsum("stywx,el->xwseytl", turn, np.eye(8)).reshape(512, 1024)
    both = np.stack([cos, sin], 0)
    fwd = np.einsum("axk,ef->aekxf", both, np.eye(8)).reshape(512, 512)
    inv = np.einsum("axk,ef->axefk", both, np.eye(8)).reshape(1024, 256)
    out = (d1, d1.T, d2, d2.T, fwd, inv, np.eye(256))
    return tuple(np.ascontiguousarray(a).astype(ml_dtypes.bfloat16) for a in out)


def dot(a, b):
    return lax.dot_general(a, b, (((1,), (0,)), ((), ())), preferred_element_type=F32)


def dot_nt(a, b):
    return lax.dot_general(a, b, (((1,), (1,)), ((), ())), preferred_element_type=F32)


def low_lanes(shape):
    return lax.broadcasted_iota(jnp.int32, shape, len(shape) - 1) < 64


def swap(v):
    return pltpu.roll(v, 64, v.ndim - 1)


def signed_swap(v, low_sign):
    turned = swap(v)
    low = low_lanes(v.shape)
    return jnp.where(low, turned, -turned) if low_sign > 0 else jnp.where(low, -turned, turned)


def stage_y(b_ref, d2_ref, s_ref):
    def one(lb, carry):
        f = dot(d2_ref[...], b_ref[lb]).reshape(32, 2, 8, 256)
        t0 = f[:, 0]
        t1 = f[:, 1]
        parts = []
        for h in range(2):
            u0 = t0[:, :, 128 * h : 128 * h + 128]
            u1 = t1[:, :, 128 * h : 128 * h + 128]
            low = low_lanes(u0.shape)
            parts.append(jnp.where(low, u0, swap(u1)))
            parts.append(jnp.where(low, swap(u0), u1))
        chunk = jnp.stack(parts, 1).reshape(32, 32, 128).astype(BF)
        s_ref[pl.ds(lb * 16, 16)] = chunk[:16]
        s_ref[pl.ds(lb * 16 + 64, 16)] = chunk[16:]
        return carry

    lax.fori_loop(0, 4, one, 0)


def unstage_y(r_ref, d2t_ref, h_ref):
    def one(lb, carry):
        r = jnp.concatenate([r_ref[pl.ds(lb * 16, 16)], r_ref[pl.ds(lb * 16 + 64, 16)]], 0)
        r = r.astype(F32).reshape(32, 4, 8, 128)
        low = low_lanes((32, 8, 128))
        t0, t1 = [], []
        for h in range(2):
            r0 = r[:, 2 * h]
            r1 = r[:, 2 * h + 1]
            t0.append(jnp.where(low, r0, swap(r1)))
            t1.append(jnp.where(low, swap(r0), r1))
        t0 = jnp.concatenate(t0, 2)
        t1 = jnp.concatenate(t1, 2)
        rows = jnp.stack([t0, t1], 1).reshape(512, 256).astype(BF)
        h_ref[lb] = dot(d2t_ref[...], rows).astype(BF)
        return carry

    lax.fori_loop(0, 4, one, 0)


def store_quad(b_ref, quad, value):
    b_ref[:, pl.ds(pl.multiple_of(quad * 64, 64), 64), :] = value.astype(BF).reshape(4, 64, 256)


def load_quad(h_ref, quad):
    return h_ref[:, pl.ds(pl.multiple_of(quad * 64, 64), 64), :].reshape(256, 256)


def columns(quad):
    return pl.ds(pl.multiple_of(quad * 256, 256), 256)


def kernel_a(v_ref, d1_ref, d2_ref, s_ref, b_ref):
    def one(quad, carry):
        store_quad(b_ref, quad, dot_nt(d1_ref[...], v_ref[:, columns(quad)]))
        return carry

    lax.fori_loop(0, 16, one, 0)
    stage_y(b_ref, d2_ref, s_ref)


def line_forward(r_ref, fwd_ref, x_ref):
    for pair in range(4):
        a = r_ref[pl.ds(32 * pair, 16)].reshape(512, 128)
        b = r_ref[pl.ds(32 * pair + 16, 16)].reshape(512, 128)
        y = dot(fwd_ref[...], jnp.concatenate([a, b], 1))
        for h in range(2):
            lanes = slice(128 * h, 128 * h + 128)
            modes = y[:256, lanes] + signed_swap(y[256:, lanes], 1)
            x_ref[pl.ds(2 * pair + h, 256, stride=8), :] = modes.astype(BF).astype(F32)


def line_inverse(p_ref, inv_ref, s_ref):
    for pair in range(4):
        a = p_ref[pl.ds(2 * pair, 256, stride=8), :].astype(BF)
        b = p_ref[pl.ds(2 * pair + 1, 256, stride=8), :].astype(BF)
        y = dot(inv_ref[...], jnp.concatenate([a, b], 1))
        for h in range(2):
            lanes = slice(128 * h, 128 * h + 128)
            lines = y[:512, lanes] + signed_swap(y[512:, lanes], -1)
            s_ref[pl.ds(32 * pair + 16 * h, 16)] = lines.astype(BF).reshape(16, 32, 128)


def mix(x_ref, w_ref, p_ref):
    row_mode = lax.broadcasted_iota(jnp.int32, (32, 128), 0) // 8
    low = low_lanes((32, 128))

    def one(group, carry):
        x = x_ref[pl.ds(pl.multiple_of(group * 32, 32), 32), :]
        xs = swap(x)
        zero = jnp.zeros_like(x)
        top, bottom = [], []
        for h in range(2):
            even = jnp.logical_and(row_mode == 2 * h, low)
            odd = jnp.logical_and(row_mode == 2 * h + 1, jnp.logical_not(low))
            top.append(jnp.where(even, x, jnp.where(odd, xs, zero)))
            bottom.append(jnp.where(even, xs, jnp.where(odd, x, zero)))
        left = jnp.concatenate(
            [jnp.concatenate(top, 1), jnp.concatenate(bottom, 1)], 0
        ).astype(BF)
        w = w_ref[pl.ds(group * 4, 4)].reshape(256, 128)
        z = dot(left, w)
        p_ref[pl.ds(pl.multiple_of(group * 32, 32), 32), :] = z[:32] + signed_swap(z[32:], -1)
        return carry

    lax.fori_loop(0, 64, one, 0, unroll=4)


def mix_back(g_ref, w_ref, p_ref):
    row_mode = lax.broadcasted_iota(jnp.int32, (32, 128), 0) // 8
    low = low_lanes((32, 128))

    def one(group, carry):
        g = g_ref[pl.ds(pl.multiple_of(group * 32, 32), 32), :]
        left = jnp.concatenate([g, signed_swap(g, 1)], 0).astype(BF)
        w = w_ref[pl.ds(group * 4, 4)].reshape(256, 128)
        z = dot_nt(left, w)
        z0, z1 = z[:32], z[32:]
        even = row_mode % 2 == 0
        first = row_mode < 2
        a0 = jnp.where(first, z0[:, :128], z0[:, 128:])
        a1 = jnp.where(first, z1[:, :128], z1[:, 128:])
        b0 = jnp.where(even, a0, swap(a0))
        b1 = jnp.where(even, swap(a1), a1)
        p_ref[pl.ds(pl.multiple_of(group * 32, 32), 32), :] = jnp.where(low, b0, b1)
        return carry

    lax.fori_loop(0, 64, one, 0, unroll=4)


def kernel_c(r_ref, w_ref, fwd_ref, inv_ref, s_ref, x_ref, p_ref):
    line_forward(r_ref, fwd_ref, x_ref)
    mix(x_ref, w_ref, p_ref)
    line_inverse(p_ref, inv_ref, s_ref)


def kernel_g(r_ref, w_ref, fwd_ref, inv_ref, s_ref, x_ref, p_ref):
    line_forward(r_ref, fwd_ref, x_ref)
    mix_back(x_ref, w_ref, p_ref)
    line_inverse(p_ref, inv_ref, s_ref)


ROOT = math.sqrt(2.0 / math.pi)


def kernel_e(
    r_ref, v_ref, cot_ref, kron_ref, bias_ref, d1_ref, d1t_ref, d2_ref, d2t_ref, eye_ref,
    s_ref, out_ref, g_ref, part_ref, h_ref, b_ref, acc_ref, sum_ref,
):
    unstage_y(r_ref, d2t_ref, h_ref)
    acc_ref[...] = jnp.zeros_like(acc_ref)
    sum_ref[...] = jnp.zeros_like(sum_ref)

    def one(quad, carry):
        eye = eye_ref[...]
        v = v_ref[:, columns(quad)]
        vt = dot_nt(eye, v).astype(BF)
        pre = dot(d1t_ref[...], load_quad(h_ref, quad)) + dot(vt, kron_ref[...]) + bias_ref[...]
        square = pre * pre
        th = jnp.tanh(ROOT * pre * (1.0 + 0.044715 * square))
        half = 0.5 + 0.5 * th
        out = (pre * half).astype(BF)
        slope = half + 0.5 * pre * (1.0 - th * th) * (ROOT + (3.0 * 0.044715 * ROOT) * square)
        cot = dot_nt(eye, cot_ref[:, columns(quad)])
        g = (cot * slope).astype(BF)
        g_ref[columns(quad), :] = g
        store_quad(b_ref, quad, dot(d1_ref[...], g))
        out_ref[:, columns(quad)] = dot_nt(eye, out).astype(BF)
        acc_ref[...] += dot(v, g)
        sum_ref[...] += jnp.sum(g.astype(F32).reshape(32, 8, 256), axis=0)
        return carry

    lax.fori_loop(0, 16, one, 0)
    stage_y(b_ref, d2_ref, s_ref)
    acc = acc_ref[...]
    low = low_lanes((64, 128))
    a = acc[:64, :128] + acc[128:192, 128:]
    b = acc[64:128, :128] + acc[192:, 128:]
    part_ref[pl.ds(0, 64), :] = jnp.where(low, a + swap(b), 0.0)
    line = jnp.sum(sum_ref[...], axis=0, keepdims=True)
    line = line[:, :128] + line[:, 128:]
    line = line + swap(line)
    part_ref[pl.ds(64, 8), :] = jnp.broadcast_to(line, (8, 128))


def kernel_i(r_ref, g_ref, kron_ref, d1t_ref, d2t_ref, eye_ref, out_ref, h_ref):
    unstage_y(r_ref, d2t_ref, h_ref)

    def one(quad, carry):
        value = dot(d1t_ref[...], load_quad(h_ref, quad)) + dot(g_ref[columns(quad), :], kron_ref[...])
        out_ref[:, columns(quad)] = dot_nt(eye_ref[...], value.astype(BF)).astype(BF)
        return carry

    lax.fori_loop(0, 16, one, 0)


def kernel_w(x_ref, g_ref, eye_ref, out_ref, a_ref):
    lane_mode = (lax.broadcasted_iota(jnp.int32, (64, 256), 1) // 8) % 16

    def one(group, carry):
        rows = pl.ds(pl.multiple_of(group * 128, 128), 128)
        xt = x_ref[rows, :].T
        xt = jnp.concatenate([xt[:64], xt[64:]], 1)
        g = g_ref[rows, :]
        right = jnp.concatenate([g, signed_swap(g, 1)], 0).astype(BF)
        left = jnp.concatenate(
            [jnp.where(lane_mode == m, xt, 0.0) for m in range(16)], 0
        ).astype(BF)
        a_ref[pl.ds(pl.multiple_of(group * 1024, 1024), 1024), :] = dot(left, right)
        return carry

    lax.fori_loop(0, 16, one, 0)

    def turn(i, carry):
        value = a_ref[pl.ds(i, 256, stride=64), :].astype(BF)
        plane = dot_nt(eye_ref[pl.ds(0, 128), pl.ds(0, 128)], value).astype(BF)
        out_ref[0, i] = plane[:64]
        out_ref[1, i] = plane[64:]
        return carry

    lax.fori_loop(0, 64, turn, 0, unroll=2)


def kernel_exchange(x_ref, o_ref, send_sem, recv_sem, local_sem):
    dp = lax.axis_index("dp")
    slab = lax.axis_index("slab")
    me = dp * SLAB + slab

    def partner(i):
        step = (i * 37) % DEVICES
        return (dp + step // SLAB) % DP, (slab + step % SLAB) % SLAB

    barrier = pltpu.get_barrier_semaphore()

    def greet(i, carry):
        pl.semaphore_signal(barrier, inc=1, device_id=partner(i), device_id_type=MESH)
        return carry

    lax.fori_loop(1, DEVICES, greet, 0)
    local = pltpu.make_async_copy(x_ref.at[me], o_ref.at[me], local_sem)
    local.start()
    pl.semaphore_wait(barrier, DEVICES - 1)

    def send(i, carry):
        to = partner(i)
        pltpu.make_async_remote_copy(
            src_ref=x_ref.at[to[0] * SLAB + to[1]],
            dst_ref=o_ref.at[me],
            send_sem=send_sem,
            recv_sem=recv_sem,
            device_id=to,
            device_id_type=MESH,
        ).start()
        return carry

    lax.fori_loop(1, DEVICES, send, 0)
    local.wait()
    rest = pl.ds(0, DEVICES - 1)
    pltpu.make_async_copy(x_ref.at[rest], x_ref.at[rest], send_sem).wait()
    pltpu.make_async_copy(o_ref.at[rest], o_ref.at[rest], recv_sem).wait()


WHOLE = pl.BlockSpec(memory_space=pltpu.VMEM)
CHUNKS = jax.ShapeDtypeStruct((DEVICES, 32, 128), BF)


def exchange(x, number):
    return pl.pallas_call(
        kernel_exchange,
        out_shape=CHUNKS,
        in_specs=[WHOLE],
        out_specs=WHOLE,
        scratch_shapes=[pltpu.SemaphoreType.DMA] * 3,
        compiler_params=pltpu.CompilerParams(collective_id=number, has_side_effects=True),
        name="exchange_%d" % number,
    )(x)


def call(kernel, out_shape, scratch, *args):
    several = isinstance(out_shape, (tuple, list))
    return pl.pallas_call(
        kernel,
        out_shape=out_shape,
        in_specs=[WHOLE] * len(args),
        out_specs=[WHOLE] * len(out_shape) if several else WHOLE,
        scratch_shapes=scratch,
        compiler_params=pltpu.CompilerParams(vmem_limit_bytes=VMEM_LIMIT),
        name=kernel.__name__,
    )(*args)


def shards(field, cotangent, spectral, skip, bias):
    d1, d1t, d2, d2t, fwd, inv, eye = (jnp.asarray(a) for a in tables())
    shape = lambda dims, dtype: jax.ShapeDtypeStruct(dims, dtype)
    half = pltpu.VMEM((4, 1024, 256), BF)
    modes = shape((2048, 128), F32)

    v = jnp.transpose(field[0], (1, 0, 2)).reshape(256, N * N)
    cot = jnp.transpose(cotangent[0], (1, 0, 2)).reshape(256, N * N)
    w = jnp.transpose(spectral, (3, 1, 0, 2)).reshape(256, C, 2 * C)
    unit = jnp.eye(4, dtype=BF)
    kron = jnp.einsum("xy,io->xiyo", unit, skip).reshape(256, 256)
    kron_back = jnp.einsum("xy,io->xoyi", unit, skip).reshape(256, 256)
    bias_row = jnp.tile(bias, 4).reshape(1, 256)

    s1 = call(kernel_a, CHUNKS, [half], v, d1, d2)
    r1 = exchange(s1, 1)
    s2, x = call(kernel_c, (CHUNKS, modes), [pltpu.VMEM((2048, 128), F32)], r1, w, fwd, inv)
    r2 = exchange(s2, 2)
    s3, out, g, part = call(
        kernel_e,
        (CHUNKS, shape((256, N * N), BF), shape((N * N, 256), BF), shape((72, 128), F32)),
        [half, half, pltpu.VMEM((256, 256), F32), pltpu.VMEM((8, 256), F32)],
        r2, v, cot, kron, bias_row, d1, d1t, d2, d2t, eye,
    )
    r3 = exchange(s3, 3)
    s4, gm = call(kernel_g, (CHUNKS, modes), [pltpu.VMEM((2048, 128), F32)], r3, w, fwd, inv)
    r4 = exchange(s4, 4)
    spectral_grad = call(
        kernel_w, shape((2, C, C, 256), BF), [pltpu.VMEM((256 * 64, 128), F32)], x, gm, eye
    )
    back = call(kernel_i, shape((256, N * N), BF), [half], r4, g, kron_back, d1t, d2t, eye)

    total = lax.psum(part[:65, :64], ("dp", "slab")) * (1.0 / math.sqrt(SAMPLES * N * N * N))
    spread = lambda a: jnp.transpose(a.reshape(4, C, N * N), (1, 0, 2))[None]
    return (spread(out), spread(back), spectral_grad, total[:64], total[64])


def solution(mesh):
    whole = P("dp", None, "slab", None)
    modes = P(None, None, None, ("slab", "dp"))
    return jax.shard_map(
        shards,
        mesh=mesh,
        in_specs=(whole, whole, modes, P(), P()),
        out_specs=(whole, whole, modes, P(), P()),
        check_vma=False,
    )
```

```python
import functools
import math

import jax
import jax.numpy as jnp
import ml_dtypes
import numpy as np
from jax import lax
from jax.experimental import pallas as pl
from jax.experimental.pallas import tpu as pltpu
from jax.sharding import PartitionSpec as P

N = 64
M = 32
C = 64
DP = 8
SLAB = 16
DEVICES = DP * SLAB
SAMPLES = 8
BF = jnp.bfloat16
F32 = jnp.float32
MESH = pl.DeviceIdType.MESH
VMEM_LIMIT = 56 * 1024 * 1024


def waves():
    phase = np.mod(np.arange(N)[:, None] * (np.arange(M)[None, :] - M // 2), N)
    angle = phase * (2.0 * math.pi / N)
    return np.cos(angle) / 8.0, np.sin(angle) / 8.0


def tables():
    cos, sin = waves()
    pair = np.stack([cos, -sin], 0).reshape(2, N, 4, 8)
    d1 = np.einsum("tzbl,uv->butlvz", pair, np.eye(4)).reshape(256, 256)
    turn = np.stack([np.stack([cos, sin], 0), np.stack([-sin, cos], 0)], 0)
    turn = turn.reshape(2, 2, N, SLAB, 2)
    d2 = np.einsum("stywx,el->xwseytl", turn, np.eye(8)).reshape(512, 1024)
    both = np.stack([cos, sin], 0)
    fwd = np.einsum("axk,ef->aekxf", both, np.eye(8)).reshape(512, 512)
    inv = np.einsum("axk,ef->axefk", both, np.eye(8)).reshape(1024, 256)
    out = (d1, d1.T, d2, d2.T, fwd, inv, np.eye(256))
    return tuple(np.ascontiguousarray(a).astype(ml_dtypes.bfloat16) for a in out)


def dot(a, b):
    return lax.dot_general(a, b, (((1,), (0,)), ((), ())), preferred_element_type=F32)


def dot_nt(a, b):
    return lax.dot_general(a, b, (((1,), (1,)), ((), ())), preferred_element_type=F32)


def low_lanes(shape):
    return lax.broadcasted_iota(jnp.int32, shape, len(shape) - 1) < 64


def swap(v):
    return pltpu.roll(v, 64, v.ndim - 1)


def signed_swap(v, low_sign):
    turned = swap(v)
    low = low_lanes(v.shape)
    return jnp.where(low, turned, -turned) if low_sign > 0 else jnp.where(low, -turned, turned)


def stage_y(b_ref, d2_ref, s_ref, first, send):
    def one(k, carry):
        lb = (first + k) % 4
        f = dot(d2_ref[...], b_ref[lb]).reshape(32, 2, 8, 256)
        t0 = f[:, 0]
        t1 = f[:, 1]
        parts = []
        for h in range(2):
            u0 = t0[:, :, 128 * h : 128 * h + 128]
            u1 = t1[:, :, 128 * h : 128 * h + 128]
            low = low_lanes(u0.shape)
            parts.append(jnp.where(low, u0, swap(u1)))
            parts.append(jnp.where(low, swap(u0), u1))
        chunk = jnp.stack(parts, 1).reshape(32, 32, 128).astype(BF)
        s_ref[pl.ds(lb * 16, 16)] = chunk[:16]
        s_ref[pl.ds(lb * 16 + 64, 16)] = chunk[16:]
        send(lb)
        send(lb + 4)
        return carry

    lax.fori_loop(0, 4, one, 0)


def unstage_y(r_ref, d2t_ref, h_ref):
    def one(lb, carry):
        r = jnp.concatenate([r_ref[pl.ds(lb * 16, 16)], r_ref[pl.ds(lb * 16 + 64, 16)]], 0)
        r = r.astype(F32).reshape(32, 4, 8, 128)
        low = low_lanes((32, 8, 128))
        t0, t1 = [], []
        for h in range(2):
            r0 = r[:, 2 * h]
            r1 = r[:, 2 * h + 1]
            t0.append(jnp.where(low, r0, swap(r1)))
            t1.append(jnp.where(low, swap(r0), r1))
        t0 = jnp.concatenate(t0, 2)
        t1 = jnp.concatenate(t1, 2)
        rows = jnp.stack([t0, t1], 1).reshape(512, 256).astype(BF)
        h_ref[lb] = dot(d2t_ref[...], rows).astype(BF)
        return carry

    lax.fori_loop(0, 4, one, 0)


def store_quad(b_ref, quad, value):
    b_ref[:, pl.ds(pl.multiple_of(quad * 64, 64), 64), :] = value.astype(BF).reshape(4, 64, 256)


def load_quad(h_ref, quad):
    return h_ref[:, pl.ds(pl.multiple_of(quad * 64, 64), 64), :].reshape(256, 256)


def columns(quad):
    return pl.ds(pl.multiple_of(quad * 256, 256), 256)


def line_forward(r_ref, fwd_ref, x_ref):
    def one(pair, carry):
        a = r_ref[pl.ds(32 * pair, 16)].reshape(512, 128)
        b = r_ref[pl.ds(32 * pair + 16, 16)].reshape(512, 128)
        y = dot(fwd_ref[...], jnp.concatenate([a, b], 1))
        for h in range(2):
            lanes = slice(128 * h, 128 * h + 128)
            modes = y[:256, lanes] + signed_swap(y[256:, lanes], 1)
            x_ref[pl.ds(2 * pair + h, 256, stride=8), :] = modes.astype(BF).astype(F32)
        return carry

    lax.fori_loop(0, 4, one, 0)


def line_inverse(p_ref, inv_ref, s_ref, first, send):
    def one(k, carry):
        pair = (first + k) % 4
        a = p_ref[pl.ds(2 * pair, 256, stride=8), :].astype(BF)
        b = p_ref[pl.ds(2 * pair + 1, 256, stride=8), :].astype(BF)
        y = dot(inv_ref[...], jnp.concatenate([a, b], 1))
        for h in range(2):
            lanes = slice(128 * h, 128 * h + 128)
            lines = y[:512, lanes] + signed_swap(y[512:, lanes], -1)
            s_ref[pl.ds(32 * pair + 16 * h, 16)] = lines.astype(BF).reshape(16, 32, 128)
        send(2 * pair)
        send(2 * pair + 1)
        return carry

    lax.fori_loop(0, 4, one, 0)


def mix(x_ref, w_ref, p_ref):
    row_mode = lax.broadcasted_iota(jnp.int32, (32, 128), 0) // 8
    low = low_lanes((32, 128))

    def one(group, carry):
        x = x_ref[pl.ds(pl.multiple_of(group * 32, 32), 32), :]
        xs = swap(x)
        zero = jnp.zeros_like(x)
        top, bottom = [], []
        for h in range(2):
            even = jnp.logical_and(row_mode == 2 * h, low)
            odd = jnp.logical_and(row_mode == 2 * h + 1, jnp.logical_not(low))
            top.append(jnp.where(even, x, jnp.where(odd, xs, zero)))
            bottom.append(jnp.where(even, xs, jnp.where(odd, x, zero)))
        left = jnp.concatenate(
            [jnp.concatenate(top, 1), jnp.concatenate(bottom, 1)], 0
        ).astype(BF)
        w = w_ref[pl.ds(pl.multiple_of(group * 256, 256), 256), :].astype(BF)
        z = dot(left, w)
        p_ref[pl.ds(pl.multiple_of(group * 32, 32), 32), :] = z[:32] + signed_swap(z[32:], -1)
        return carry

    lax.fori_loop(0, 64, one, 0, unroll=4)


def mix_back(g_ref, w_ref, p_ref):
    row_mode = lax.broadcasted_iota(jnp.int32, (32, 128), 0) // 8
    low = low_lanes((32, 128))

    def one(group, carry):
        g = g_ref[pl.ds(pl.multiple_of(group * 32, 32), 32), :]
        left = jnp.concatenate([g, signed_swap(g, 1)], 0).astype(BF)
        w = w_ref[pl.ds(pl.multiple_of(group * 256, 256), 256), :].astype(BF)
        z = dot_nt(left, w)
        z0, z1 = z[:32], z[32:]
        even = row_mode % 2 == 0
        first = row_mode < 2
        a0 = jnp.where(first, z0[:, :128], z0[:, 128:])
        a1 = jnp.where(first, z1[:, :128], z1[:, 128:])
        b0 = jnp.where(even, a0, swap(a0))
        b1 = jnp.where(even, swap(a1), a1)
        p_ref[pl.ds(pl.multiple_of(group * 32, 32), 32), :] = jnp.where(low, b0, b1)
        return carry

    lax.fori_loop(0, 64, one, 0, unroll=4)


ROOT = math.sqrt(2.0 / math.pi)
FACTOR = 1.0 / math.sqrt(SAMPLES * N * N * N)


def turn_weights(raw_ref, eye_ref, w_ref):
    def one(i, carry):
        plane = jnp.concatenate([raw_ref[0, i], raw_ref[1, i]], 0)
        w_ref[pl.ds(i, 256, stride=64), :] = dot_nt(eye_ref[...], plane)
        return carry

    lax.fori_loop(0, 64, one, 0, unroll=2)


def weight_gradient(x_ref, g_ref, eye_ref, out_ref, a_ref):
    lane_mode = (lax.broadcasted_iota(jnp.int32, (64, 256), 1) // 8) % 16

    def one(group, carry):
        rows = pl.ds(pl.multiple_of(group * 128, 128), 128)
        xt = x_ref[rows, :].T
        xt = jnp.concatenate([xt[:64], xt[64:]], 1)
        g = g_ref[rows, :]
        right = jnp.concatenate([g, signed_swap(g, 1)], 0).astype(BF)
        left = jnp.concatenate(
            [jnp.where(lane_mode == m, xt, 0.0) for m in range(16)], 0
        ).astype(BF)
        a_ref[pl.ds(pl.multiple_of(group * 1024, 1024), 1024), :] = dot(left, right)
        return carry

    lax.fori_loop(0, 16, one, 0)

    def turn(i, carry):
        value = a_ref[pl.ds(i, 256, stride=64), :].astype(BF)
        plane = dot_nt(eye_ref[pl.ds(0, 128), pl.ds(0, 128)], value).astype(BF)
        out_ref[0, i] = plane[:64]
        out_ref[1, i] = plane[64:]
        return carry

    lax.fori_loop(0, 64, turn, 0, unroll=2)


def layer(
    v_ref, cot_hbm, raw_hbm, kron_ref, kron_back_ref, bias_ref,
    d1_ref, d1t_ref, d2_ref, d2t_ref, fwd_ref, inv_ref, eye_ref,
    out_hbm, back_ref, sg_hbm, skip_ref, line_ref,
    cot_ref, raw_ref, out_ref, sg_ref, g_ref, h_ref, b_ref, w_ref, x_ref, y_ref, p_ref,
    acc_ref, sum_ref, part_ref, slab_ref, half_ref, dp_ref, total_ref,
    s1, s2, r1, r2, r3, r4,
    send_sem, recv_sem, local_sem, load_sem, store_sem, small_send, small_recv,
):
    dp = lax.axis_index("dp")
    slab = lax.axis_index("slab")
    me = dp * SLAB + slab

    def wait_bytes(ref, sem):
        pltpu.make_async_copy(ref, ref, sem).wait()

    barrier = pltpu.get_barrier_semaphore()

    def greet(i, carry):
        to = ((dp + i // SLAB) % DP, (slab + i % SLAB) % SLAB)
        pl.semaphore_signal(barrier, inc=1, device_id=to, device_id_type=MESH)
        return carry

    lax.fori_loop(1, DEVICES, greet, 0)
    load_cot = pltpu.make_async_copy(cot_hbm, cot_ref, load_sem.at[0])
    load_raw = pltpu.make_async_copy(raw_hbm, raw_ref, load_sem.at[1])
    load_raw.start()
    load_cot.start()

    def sender(s_ref, r_ref, phase):
        def remote(row, step):
            column = (slab + step) % SLAB
            return pltpu.make_async_remote_copy(
                src_ref=s_ref.at[row * SLAB + column],
                dst_ref=r_ref.at[me],
                send_sem=send_sem.at[phase],
                recv_sem=recv_sem.at[phase],
                device_id=(row, column),
                device_id_type=MESH,
            )

        def send(row):
            def one(step, carry):
                remote(row, step).start()
                return carry

            lax.fori_loop(1, SLAB, one, 0)

            @pl.when(row != dp)
            def _():
                remote(row, 0).start()

            @pl.when(row == dp)
            def _():
                pltpu.make_async_copy(s_ref.at[me], r_ref.at[me], local_sem.at[phase]).start()

        return send

    rest = pl.ds(0, DEVICES - 1)

    def arrived(s_ref, r_ref, phase):
        pltpu.make_async_copy(s_ref.at[me], r_ref.at[me], local_sem.at[phase]).wait()
        wait_bytes(s_ref.at[rest], send_sem.at[phase])
        wait_bytes(r_ref.at[rest], recv_sem.at[phase])

    def plane_one(quad, carry):
        store_quad(b_ref, quad, dot_nt(d1_ref[...], v_ref[:, columns(quad)]))
        return carry

    lax.fori_loop(0, 16, plane_one, 0)
    pl.semaphore_wait(barrier, DEVICES - 1)
    stage_y(b_ref, d2_ref, s1, dp % 4, sender(s1, r1, 0))
    load_raw.wait()
    turn_weights(raw_ref, eye_ref, w_ref)
    load_cot.wait()
    arrived(s1, r1, 0)

    line_forward(r1, fwd_ref, x_ref)
    mix(x_ref, w_ref, p_ref)
    line_inverse(p_ref, inv_ref, s2, dp // 2, sender(s2, r2, 1))
    arrived(s2, r2, 1)

    unstage_y(r2, d2t_ref, h_ref)
    acc_ref[...] = jnp.zeros_like(acc_ref)
    sum_ref[...] = jnp.zeros_like(sum_ref)

    def point(quad, carry):
        eye = eye_ref[...]
        v = v_ref[:, columns(quad)]
        vt = dot_nt(eye, v).astype(BF)
        pre = dot(d1t_ref[...], load_quad(h_ref, quad)) + dot(vt, kron_ref[...]) + bias_ref[...]
        square = pre * pre
        th = jnp.tanh(ROOT * pre * (1.0 + 0.044715 * square))
        half = 0.5 + 0.5 * th
        out = (pre * half).astype(BF)
        slope = half + 0.5 * pre * (1.0 - th * th) * (ROOT + (3.0 * 0.044715 * ROOT) * square)
        cot = dot_nt(eye, cot_ref[:, columns(quad)])
        g = (cot * slope).astype(BF)
        g_ref[columns(quad), :] = g
        store_quad(b_ref, quad, dot(d1_ref[...], g))
        out_ref[:, columns(quad)] = dot_nt(eye, out).astype(BF)
        return carry

    lax.fori_loop(0, 16, point, 0)
    stage_y(b_ref, d2_ref, s1, dp % 4, sender(s1, r3, 2))
    store_out = pltpu.make_async_copy(out_ref, out_hbm, store_sem.at[0])
    store_out.start()

    def outer(quad, carry):
        g = g_ref[columns(quad), :]
        acc_ref[...] += dot(v_ref[:, columns(quad)], g)
        sum_ref[...] += jnp.sum(g.astype(F32).reshape(32, 8, 256), axis=0)
        return carry

    lax.fori_loop(0, 16, outer, 0)
    acc = acc_ref[...]
    low = low_lanes((64, 128))
    a = acc[:64, :128] + acc[128:192, 128:]
    b = acc[64:128, :128] + acc[192:, 128:]
    part_ref[pl.ds(0, 8)] = jnp.where(low, a + swap(b), 0.0).reshape(8, 8, 128)
    line = jnp.sum(sum_ref[...], axis=0, keepdims=True)
    line = line[:, :128] + line[:, 128:]
    line = line + swap(line)
    part_ref[8] = jnp.broadcast_to(line, (8, 128))
    part_ref[pl.ds(9, 7)] = jnp.zeros((7, 8, 128), F32)

    def along_slab(source, target_ref, at, number):
        def one(step, carry):
            column = (slab + step) % SLAB
            pltpu.make_async_remote_copy(
                src_ref=source(column),
                dst_ref=target_ref.at[at],
                send_sem=small_send.at[number],
                recv_sem=small_recv.at[number],
                device_id=(dp, column),
                device_id_type=MESH,
            ).start()
            return carry

        lax.fori_loop(1, SLAB, one, 0)

    few = pl.ds(0, SLAB - 1)
    along_slab(lambda column: part_ref.at[column], slab_ref, slab, 0)
    arrived(s1, r3, 2)
    wait_bytes(part_ref.at[few], small_send.at[0])
    wait_bytes(slab_ref.at[few], small_recv.at[0])
    slab_ref[slab] = part_ref[slab]
    half_ref[...] = jnp.sum(slab_ref[...], axis=0)

    def along_dp(step, carry):
        pltpu.make_async_remote_copy(
            src_ref=half_ref,
            dst_ref=dp_ref.at[dp],
            send_sem=small_send.at[1],
            recv_sem=small_recv.at[1],
            device_id=((dp + step) % DP, slab),
            device_id_type=MESH,
        ).start()
        return carry

    lax.fori_loop(1, DP, along_dp, 0)

    line_forward(r3, fwd_ref, y_ref)
    mix_back(y_ref, w_ref, p_ref)
    line_inverse(p_ref, inv_ref, s2, dp // 2, sender(s2, r4, 3))

    seven = pl.ds(0, DP - 1)
    wait_bytes(dp_ref.at[seven], small_send.at[1])
    wait_bytes(dp_ref.at[seven], small_recv.at[1])
    dp_ref[dp] = half_ref[...]
    part_ref[slab] = jnp.sum(dp_ref[...], axis=0) * FACTOR
    total_ref[slab] = part_ref[slab]
    along_slab(lambda column: part_ref.at[slab], total_ref, slab, 2)

    weight_gradient(x_ref, y_ref, eye_ref, sg_ref, w_ref)
    store_sg = pltpu.make_async_copy(sg_ref, sg_hbm, store_sem.at[1])
    store_sg.start()
    wait_bytes(part_ref.at[few], small_send.at[2])
    wait_bytes(total_ref.at[few], small_recv.at[2])
    skip_ref[...] = total_ref[pl.ds(0, 8)].reshape(64, 128)[:, :64]
    line_ref[...] = total_ref[8][:1, :64]
    arrived(s2, r4, 3)

    unstage_y(r4, d2t_ref, h_ref)

    def last(quad, carry):
        value = dot(d1t_ref[...], load_quad(h_ref, quad)) + dot(g_ref[columns(quad), :], kron_back_ref[...])
        back_ref[:, columns(quad)] = dot_nt(eye_ref[...], value.astype(BF)).astype(BF)
        return carry

    lax.fori_loop(0, 16, last, 0)
    store_out.wait()
    store_sg.wait()


WHOLE = pl.BlockSpec(memory_space=pltpu.VMEM)
AWAY = pl.BlockSpec(memory_space=pl.ANY)


def shards(field, cotangent, spectral, skip, bias):
    d1, d1t, d2, d2t, fwd, inv, eye = (jnp.asarray(a) for a in tables())
    shape = lambda dims, dtype: jax.ShapeDtypeStruct(dims, dtype)
    v = jnp.transpose(field[0], (1, 0, 2)).reshape(256, N * N)
    cot = jnp.transpose(cotangent[0], (1, 0, 2)).reshape(256, N * N)
    unit = jnp.eye(4, dtype=BF)
    kron = jnp.einsum("xy,io->xiyo", unit, skip).reshape(256, 256)
    kron_back = jnp.einsum("xy,io->xoyi", unit, skip).reshape(256, 256)
    bias_row = jnp.tile(bias, 4).reshape(1, 256)
    half = pltpu.VMEM((4, 1024, 256), BF)
    grid = pltpu.VMEM((256, N * N), BF)
    modes = pltpu.VMEM((2048, 128), F32)
    weights = pltpu.VMEM((2, C, C, 256), BF)
    chunks = pltpu.VMEM((DEVICES, 32, 128), BF)
    small = lambda count: pltpu.VMEM((count, 8, 128), F32)
    dma = pltpu.SemaphoreType.DMA
    out, back, spectral_grad, skip_grad, bias_grad = pl.pallas_call(
        layer,
        out_shape=(
            shape((256, N * N), BF),
            shape((256, N * N), BF),
            shape((2, C, C, 256), BF),
            shape((C, C), F32),
            shape((1, C), F32),
        ),
        in_specs=[WHOLE, AWAY, AWAY] + [WHOLE] * 10,
        out_specs=[AWAY, WHOLE, AWAY, WHOLE, WHOLE],
        scratch_shapes=[
            grid, weights, grid, weights, pltpu.VMEM((N * N, 256), BF), half, half,
            pltpu.VMEM((256 * 64, 128), F32), modes, modes, modes,
            pltpu.VMEM((256, 256), F32), pltpu.VMEM((8, 256), F32),
            small(16), small(16), pltpu.VMEM((8, 128), F32), small(8), small(16),
        ]
        + [chunks] * 6
        + [dma((4,)), dma((4,)), dma((4,)), dma((2,)), dma((2,)), dma((3,)), dma((3,))],
        compiler_params=pltpu.CompilerParams(
            collective_id=1, has_side_effects=True, vmem_limit_bytes=VMEM_LIMIT
        ),
        name="layer",
    )(v, cot, spectral, kron, kron_back, bias_row, d1, d1t, d2, d2t, fwd, inv, eye)
    spread = lambda a: jnp.transpose(a.reshape(4, C, N * N), (1, 0, 2))[None]
    return (spread(out), spread(back), spectral_grad, skip_grad, bias_grad[0])


def solution(mesh):
    whole = P("dp", None, "slab", None)
    modes = P(None, None, None, ("slab", "dp"))
    return jax.shard_map(
        shards,
        mesh=mesh,
        in_specs=(whole, whole, modes, P(), P()),
        out_specs=(whole, whole, modes, P(), P()),
        check_vma=False,
    )
```

```python
import functools
import math

import jax
import jax.numpy as jnp
import ml_dtypes
import numpy as np
from jax import lax
from jax.experimental import pallas as pl
from jax.experimental.pallas import tpu as pltpu
from jax.sharding import PartitionSpec as P

N = 64
M = 32
C = 64
DP = 8
SLAB = 16
DEVICES = DP * SLAB
SAMPLES = 8
BF = jnp.bfloat16
F32 = jnp.float32
MESH = pl.DeviceIdType.MESH
VMEM_LIMIT = 56 * 1024 * 1024


def waves():
    phase = np.mod(np.arange(N)[:, None] * (np.arange(M)[None, :] - M // 2), N)
    angle = phase * (2.0 * math.pi / N)
    return np.cos(angle) / 8.0, np.sin(angle) / 8.0


def tables():
    cos, sin = waves()
    pair = np.stack([cos, -sin], 0).reshape(2, N, 4, 2, 4)
    d1 = np.einsum("tzbhl,uv->hbutlvz", pair, np.eye(4)).reshape(256, 256)
    turn = np.stack([np.stack([cos, sin], 0), np.stack([-sin, cos], 0)], 0)
    turn = turn.reshape(2, 2, N, SLAB, 2)
    d2 = np.einsum("stywx,el->xwseytl", turn, np.eye(4)).reshape(256, 512)
    both = np.stack([cos, sin], 0)
    fwd = np.einsum("axk,ef->aekxf", both, np.eye(4)).reshape(256, 256)
    inv = np.einsum("axk,ef->axefk", both, np.eye(4)).reshape(512, 128)
    eye = np.eye(256)
    order = np.eye(256).reshape(64, 4, 256).transpose(1, 0, 2).reshape(256, 256)
    repeat = np.tile(np.eye(64), (4, 1))
    out = (d1, d1.T, d2, d2.T, fwd, inv, eye, order, order.T, repeat)
    return tuple(np.ascontiguousarray(a).astype(ml_dtypes.bfloat16) for a in out)


def dot(a, b):
    return lax.dot_general(a, b, (((1,), (0,)), ((), ())), preferred_element_type=F32)


def dot_nt(a, b):
    return lax.dot_general(a, b, (((1,), (1,)), ((), ())), preferred_element_type=F32)


def low_lanes(shape):
    return lax.broadcasted_iota(jnp.int32, shape, len(shape) - 1) < 64


def swap(v):
    return pltpu.roll(v, 64, v.ndim - 1)


def signed_swap(v, low_sign):
    turned = swap(v)
    low = low_lanes(v.shape)
    return jnp.where(low, turned, -turned) if low_sign > 0 else jnp.where(low, -turned, turned)


def cross(v):
    upper = lax.broadcasted_iota(jnp.int32, v.shape, v.ndim - 2) < 4
    keep = upper == low_lanes(v.shape)
    return jnp.where(keep, v, swap(pltpu.roll(v, 4, v.ndim - 2)))


def rows_apart(w):
    w = w.reshape(32, 2, 8, 128)
    even, odd = w[:, 0], w[:, 1]
    upper = lax.broadcasted_iota(jnp.int32, even.shape, 1) < 4
    first = jnp.where(upper, even, pltpu.roll(odd, 4, 1))
    second = jnp.where(upper, pltpu.roll(even, 4, 1), odd)
    return jnp.concatenate([first.reshape(256, 128), second.reshape(256, 128)], 1)


def rows_together(value):
    first = value[:, :128].reshape(32, 8, 128)
    second = value[:, 128:].reshape(32, 8, 128)
    upper = lax.broadcasted_iota(jnp.int32, first.shape, 1) < 4
    even = jnp.where(upper, first, pltpu.roll(second, 4, 1))
    odd = jnp.where(upper, pltpu.roll(first, 4, 1), second)
    return jnp.stack([even, odd], 1).reshape(64, 8, 128)


def sixteen(index):
    return pl.ds(pl.multiple_of(index * 16, 16), 16)


def stage_y(b_ref, d2_ref, s_ref, half):
    def one(lb, carry):
        f = dot(d2_ref[...], b_ref[half * 4 + lb]).reshape(32, 8, 256)
        chunk = jnp.concatenate([cross(f[:, :, :128]), cross(f[:, :, 128:])], 1).astype(BF)
        s_ref[half, pl.ds(lb * 16, 16)] = chunk[:16]
        s_ref[half, pl.ds(lb * 16 + 64, 16)] = chunk[16:]
        return carry

    lax.fori_loop(0, 4, one, 0, unroll=True)


def unstage_y(r_ref, d2t_ref, h_ref, half):
    def one(lb, carry):
        r = jnp.concatenate(
            [r_ref[half, pl.ds(lb * 16, 16)], r_ref[half, pl.ds(lb * 16 + 64, 16)]], 0
        ).astype(F32)
        rows = jnp.concatenate([cross(r[:, :8]), cross(r[:, 8:])], 2).reshape(256, 256)
        h_ref[half * 4 + lb] = dot(d2t_ref[...], rows.astype(BF)).astype(BF)
        return carry

    lax.fori_loop(0, 4, one, 0, unroll=True)


def store_quad(b_ref, quad, value):
    b_ref[:, pl.ds(pl.multiple_of(quad * 32, 32), 32), :] = value.astype(BF).reshape(8, 32, 256)


def load_quad(h_ref, quad):
    return h_ref[:, pl.ds(pl.multiple_of(quad * 32, 32), 32), :].reshape(256, 256)


def columns(quad):
    return pl.ds(pl.multiple_of(quad * 256, 256), 256)


def line_forward(r_ref, fwd_ref, x_ref, half):
    def one(pair, carry):
        a = r_ref[half, pl.ds(32 * pair, 16)].reshape(256, 128)
        b = r_ref[half, pl.ds(32 * pair + 16, 16)].reshape(256, 128)
        y = dot(fwd_ref[...], jnp.concatenate([a, b], 1))
        for h in range(2):
            lanes = slice(128 * h, 128 * h + 128)
            modes = y[:128, lanes] + signed_swap(y[128:, lanes], 1)
            x_ref[pl.ds(1024 * half + 2 * pair + h, 128, stride=8), :] = modes.astype(BF).astype(F32)
        return carry

    lax.fori_loop(0, 4, one, 0, unroll=True)


def line_inverse(p_ref, inv_ref, s_ref, half):
    def one(pair, carry):
        a = p_ref[pl.ds(1024 * half + 2 * pair, 128, stride=8), :].astype(BF)
        b = p_ref[pl.ds(1024 * half + 2 * pair + 1, 128, stride=8), :].astype(BF)
        y = dot(inv_ref[...], jnp.concatenate([a, b], 1))
        for h in range(2):
            lanes = slice(128 * h, 128 * h + 128)
            lines = y[:256, lanes] + signed_swap(y[256:, lanes], -1)
            s_ref[half, pl.ds(32 * pair + 16 * h, 16)] = lines.astype(BF).reshape(16, 16, 128)
        return carry

    lax.fori_loop(0, 4, one, 0, unroll=True)


def mix(x_ref, w_ref, p_ref, half):
    row_mode = lax.broadcasted_iota(jnp.int32, (32, 128), 0) // 8
    low = low_lanes((32, 128))

    def one(group, carry):
        x = x_ref[pl.ds(pl.multiple_of(group * 32, 32), 32), :]
        xs = swap(x)
        zero = jnp.zeros_like(x)
        top, bottom = [], []
        for h in range(2):
            even = jnp.logical_and(row_mode == 2 * h, low)
            odd = jnp.logical_and(row_mode == 2 * h + 1, jnp.logical_not(low))
            top.append(jnp.where(even, x, jnp.where(odd, xs, zero)))
            bottom.append(jnp.where(even, xs, jnp.where(odd, x, zero)))
        left = jnp.concatenate(
            [jnp.concatenate(top, 1), jnp.concatenate(bottom, 1)], 0
        ).astype(BF)
        w = w_ref[pl.ds(pl.multiple_of(group * 256, 256), 256), :].astype(BF)
        z = dot(left, w)
        p_ref[pl.ds(pl.multiple_of(group * 32, 32), 32), :] = z[:32] + signed_swap(z[32:], -1)
        return carry

    lax.fori_loop(32 * half, 32 * half + 32, one, 0, unroll=4)


def mix_back(g_ref, w_ref, p_ref, half):
    row_mode = lax.broadcasted_iota(jnp.int32, (32, 128), 0) // 8
    low = low_lanes((32, 128))

    def one(group, carry):
        g = g_ref[pl.ds(pl.multiple_of(group * 32, 32), 32), :]
        left = jnp.concatenate([g, signed_swap(g, 1)], 0).astype(BF)
        w = w_ref[pl.ds(pl.multiple_of(group * 256, 256), 256), :].astype(BF)
        z = dot_nt(left, w)
        z0, z1 = z[:32], z[32:]
        even = row_mode % 2 == 0
        first = row_mode < 2
        a0 = jnp.where(first, z0[:, :128], z0[:, 128:])
        a1 = jnp.where(first, z1[:, :128], z1[:, 128:])
        b0 = jnp.where(even, a0, swap(a0))
        b1 = jnp.where(even, swap(a1), a1)
        p_ref[pl.ds(pl.multiple_of(group * 32, 32), 32), :] = jnp.where(low, b0, b1)
        return carry

    lax.fori_loop(32 * half, 32 * half + 32, one, 0, unroll=4)


ROOT = math.sqrt(2.0 / math.pi)
FACTOR = 1.0 / math.sqrt(SAMPLES * N * N * N)


def turn_weights(raw_ref, eye_ref, w_ref, half):
    lanes = slice(128 * half, 128 * half + 128)

    def one(i, carry):
        plane = jnp.concatenate([raw_ref[0, i, :, lanes], raw_ref[1, i, :, lanes]], 0)
        turned = dot_nt(eye_ref[pl.ds(0, 128), pl.ds(0, 128)], plane)
        w_ref[pl.ds(8192 * half + i, 128, stride=64), :] = turned
        return carry

    lax.fori_loop(0, 64, one, 0, unroll=4)


def weight_gradient(x_ref, g_ref, eye_ref, out_ref, a_ref):
    lane_mode = (lax.broadcasted_iota(jnp.int32, (64, 256), 1) // 8) % 16

    def one(group, carry):
        rows = pl.ds(pl.multiple_of(group * 128, 128), 128)
        xt = x_ref[rows, :].T
        xt = jnp.concatenate([xt[:64], xt[64:]], 1)
        g = g_ref[rows, :]
        right = jnp.concatenate([g, signed_swap(g, 1)], 0).astype(BF)
        left = jnp.concatenate(
            [jnp.where(lane_mode == m, xt, 0.0) for m in range(16)], 0
        ).astype(BF)
        a_ref[pl.ds(pl.multiple_of(group * 1024, 1024), 1024), :] = dot(left, right)
        return carry

    lax.fori_loop(0, 16, one, 0)

    def turn(i, carry):
        value = a_ref[pl.ds(i, 256, stride=64), :].astype(BF)
        plane = dot_nt(eye_ref[pl.ds(0, 128), pl.ds(0, 128)], value).astype(BF)
        out_ref[0, i] = plane[:64]
        out_ref[1, i] = plane[64:]
        return carry

    lax.fori_loop(0, 64, turn, 0, unroll=2)


def layer(
    field_hbm, cot_hbm, raw_hbm, skip_in, bias_in,
    d1_ref, d1t_ref, d2_ref, d2t_ref, fwd_ref, inv_ref, eye_ref, order_ref, back_order_ref, repeat_ref,
    out_hbm, back_hbm, sg_hbm, skip_ref, line_ref,
    io_ref, cot_ref, raw_ref, v_ref, ct_ref, out_ref, g_ref, vk_ref, h_ref, b_ref, w_ref,
    x_ref, y_ref, p_ref, kron_ref,
    acc_ref, sum_ref, part_ref, slab_ref, half_ref, dp_ref, total_ref,
    s1, s2, r1, r2, r3, r4,
    send_sem, recv_sem, local_sem, load_sem, store_sem, small_send, small_recv,
):
    dp = lax.axis_index("dp")
    slab = lax.axis_index("slab")
    me = dp * SLAB + slab

    def wait_bytes(ref, sem):
        pltpu.make_async_copy(ref, ref, sem).wait()

    def partner(i):
        step = (i * 37) % DEVICES
        return (dp + step // SLAB) % DP, (slab + step % SLAB) % SLAB

    barrier = pltpu.get_barrier_semaphore()
    load_field = pltpu.make_async_copy(field_hbm, io_ref, load_sem.at[0])
    load_raw = pltpu.make_async_copy(raw_hbm, raw_ref, load_sem.at[1])
    load_cot = pltpu.make_async_copy(cot_hbm, cot_ref, load_sem.at[2])
    load_field.start()
    load_raw.start()
    load_cot.start()

    def greet(i, carry):
        pl.semaphore_signal(barrier, inc=1, device_id=partner(i), device_id_type=MESH)
        return carry

    lax.fori_loop(1, DEVICES, greet, 0)

    rest = pl.ds(0, DEVICES - 1)

    def send(s_ref, r_ref, phase, half):
        at = 2 * phase + half
        pltpu.make_async_copy(s_ref.at[half, me], r_ref.at[half, me], local_sem.at[at]).start()

        def one(i, carry):
            to = partner(i)
            pltpu.make_async_remote_copy(
                src_ref=s_ref.at[half, to[0] * SLAB + to[1]],
                dst_ref=r_ref.at[half, me],
                send_sem=send_sem.at[at],
                recv_sem=recv_sem.at[at],
                device_id=to,
                device_id_type=MESH,
            ).start()
            return carry

        lax.fori_loop(1, DEVICES, one, 0)

    def arrived(s_ref, r_ref, phase, half):
        at = 2 * phase + half
        pltpu.make_async_copy(s_ref.at[half, me], r_ref.at[half, me], local_sem.at[at]).wait()
        wait_bytes(r_ref.at[half, rest], recv_sem.at[at])

    def sent(s_ref, phase):
        for half in range(2):
            wait_bytes(s_ref.at[half, rest], send_sem.at[2 * phase + half])

    wide = dot_nt(dot(repeat_ref[...], skip_in[...]).astype(BF), repeat_ref[...])
    same = (
        lax.broadcasted_iota(jnp.int32, (256, 256), 0) // 64
        == lax.broadcasted_iota(jnp.int32, (256, 256), 1) // 64
    )
    kron_ref[...] = jnp.where(same, wide, 0.0).astype(BF)
    bias = jnp.concatenate([bias_in[...]] * 4, 1)

    load_field.wait()

    def plane_one(index, carry):
        block = io_ref[:, sixteen(index), :].astype(F32)
        for j in range(2):
            v = rows_apart(block[:, 8 * j : 8 * j + 8]).astype(BF)
            v = dot(order_ref[...], v).astype(BF)
            v_ref[:, columns(2 * index + j)] = v
            store_quad(b_ref, 2 * index + j, dot_nt(d1_ref[...], v))
        return carry

    lax.fori_loop(0, 8, plane_one, 0)
    stage_y(b_ref, d2_ref, s1, 0)
    pl.semaphore_wait(barrier, DEVICES - 1)
    send(s1, r1, 0, 0)
    stage_y(b_ref, d2_ref, s1, 1)
    send(s1, r1, 0, 1)
    load_raw.wait()

    for half in range(2):
        turn_weights(raw_ref, eye_ref, w_ref, half)
        arrived(s1, r1, 0, half)
        line_forward(r1, fwd_ref, x_ref, half)
        mix(x_ref, w_ref, p_ref, half)
        line_inverse(p_ref, inv_ref, s2, half)
        send(s2, r2, 1, half)

    load_cot.wait()

    def prepare(index, carry):
        block = cot_ref[:, sixteen(index), :].astype(F32)
        for j in range(2):
            quad = columns(2 * index + j)
            cot = rows_apart(block[:, 8 * j : 8 * j + 8]).astype(BF)
            cot = dot(order_ref[...], cot).astype(BF)
            ct_ref[quad, :] = dot_nt(eye_ref[...], cot).astype(BF)
            vt = dot_nt(eye_ref[...], v_ref[:, quad]).astype(BF)
            vk_ref[quad, :] = dot(vt, kron_ref[...]) + bias
        return carry

    lax.fori_loop(0, 8, prepare, 0)
    for half in range(2):
        arrived(s2, r2, 1, half)
        unstage_y(r2, d2t_ref, h_ref, half)

    def point(index, carry):
        for j in range(2):
            quad = 2 * index + j
            pre = dot(d1t_ref[...], load_quad(h_ref, quad)) + vk_ref[columns(quad), :]
            square = pre * pre
            th = jnp.tanh(ROOT * pre * (1.0 + 0.044715 * square))
            half = 0.5 + 0.5 * th
            out_ref[columns(quad), :] = (pre * half).astype(BF)
            slope = half + 0.5 * pre * (1.0 - th * th) * (ROOT + (3.0 * 0.044715 * ROOT) * square)
            g = (ct_ref[columns(quad), :].astype(F32) * slope).astype(BF)
            g_ref[columns(quad), :] = g
            store_quad(b_ref, quad, dot(d1_ref[...], g))
        return carry

    lax.fori_loop(0, 8, point, 0)
    sent(s1, 0)
    for half in range(2):
        stage_y(b_ref, d2_ref, s1, half)
        send(s1, r3, 2, half)

    acc_ref[...] = jnp.zeros_like(acc_ref)
    sum_ref[...] = jnp.zeros_like(sum_ref)

    def outer(quad, carry):
        g = g_ref[columns(quad), :]
        acc_ref[...] += dot(v_ref[:, columns(quad)], g)
        sum_ref[...] += jnp.sum(g.astype(F32).reshape(32, 8, 256), axis=0)
        return carry

    lax.fori_loop(0, 16, outer, 0, unroll=2)
    acc = acc_ref[...]
    low = low_lanes((64, 128))
    a = acc[:64, :128] + acc[128:192, 128:]
    b = acc[64:128, :128] + acc[192:, 128:]
    part_ref[pl.ds(0, 8)] = jnp.where(low, a + swap(b), 0.0).reshape(8, 8, 128)
    line = jnp.sum(sum_ref[...], axis=0, keepdims=True)
    line = line[:, :128] + line[:, 128:]
    line = line + swap(line)
    part_ref[8] = jnp.broadcast_to(line, (8, 128))
    part_ref[pl.ds(9, 7)] = jnp.zeros((7, 8, 128), F32)

    def along_slab(source, target_ref, at, number):
        def one(step, carry):
            column = (slab + step) % SLAB
            pltpu.make_async_remote_copy(
                src_ref=source(column),
                dst_ref=target_ref.at[at],
                send_sem=small_send.at[number],
                recv_sem=small_recv.at[number],
                device_id=(dp, column),
                device_id_type=MESH,
            ).start()
            return carry

        lax.fori_loop(1, SLAB, one, 0)

    few = pl.ds(0, SLAB - 1)
    along_slab(lambda column: part_ref.at[column], slab_ref, slab, 0)

    def turn_out(index, carry):
        both = []
        for j in range(2):
            both.append(rows_together(dot_nt(back_order_ref[...], out_ref[columns(2 * index + j), :])))
        io_ref[:, sixteen(index), :] = jnp.concatenate(both, 1).astype(BF)
        return carry

    lax.fori_loop(0, 8, turn_out, 0)
    store_out = pltpu.make_async_copy(io_ref, out_hbm, store_sem.at[0])
    store_out.start()

    sent(s2, 1)
    for half in range(2):
        arrived(s1, r3, 2, half)
        line_forward(r3, fwd_ref, y_ref, half)
        mix_back(y_ref, w_ref, p_ref, half)
        line_inverse(p_ref, inv_ref, s2, half)
        send(s2, r4, 3, half)

    wait_bytes(part_ref.at[few], small_send.at[0])
    wait_bytes(slab_ref.at[few], small_recv.at[0])
    slab_ref[slab] = part_ref[slab]
    half_ref[...] = jnp.sum(slab_ref[...], axis=0)

    def along_dp(step, carry):
        pltpu.make_async_remote_copy(
            src_ref=half_ref,
            dst_ref=dp_ref.at[dp],
            send_sem=small_send.at[1],
            recv_sem=small_recv.at[1],
            device_id=((dp + step) % DP, slab),
            device_id_type=MESH,
        ).start()
        return carry

    lax.fori_loop(1, DP, along_dp, 0)
    weight_gradient(x_ref, y_ref, eye_ref, raw_ref, w_ref)
    store_sg = pltpu.make_async_copy(raw_ref, sg_hbm, store_sem.at[1])
    store_sg.start()

    seven = pl.ds(0, DP - 1)
    wait_bytes(dp_ref.at[seven], small_send.at[1])
    wait_bytes(dp_ref.at[seven], small_recv.at[1])
    dp_ref[dp] = half_ref[...]
    part_ref[slab] = jnp.sum(dp_ref[...], axis=0) * FACTOR
    total_ref[slab] = part_ref[slab]
    along_slab(lambda column: part_ref.at[slab], total_ref, slab, 2)

    def skip_back(quad, carry):
        vk_ref[columns(quad), :] = dot_nt(g_ref[columns(quad), :], kron_ref[...])
        return carry

    lax.fori_loop(0, 16, skip_back, 0, unroll=2)
    for half in range(2):
        arrived(s2, r4, 3, half)
        unstage_y(r4, d2t_ref, h_ref, half)

    def last(index, carry):
        both = []
        for j in range(2):
            quad = 2 * index + j
            value = dot(d1t_ref[...], load_quad(h_ref, quad)) + vk_ref[columns(quad), :]
            both.append(rows_together(dot_nt(back_order_ref[...], value.astype(BF))))
        cot_ref[:, sixteen(index), :] = jnp.concatenate(both, 1).astype(BF)
        return carry

    lax.fori_loop(0, 8, last, 0)
    store_back = pltpu.make_async_copy(cot_ref, back_hbm, store_sem.at[2])
    store_back.start()
    sent(s1, 2)
    sent(s2, 3)
    wait_bytes(part_ref.at[few], small_send.at[2])
    wait_bytes(total_ref.at[few], small_recv.at[2])
    skip_ref[...] = total_ref[pl.ds(0, 8)].reshape(64, 128)[:, :64]
    line_ref[...] = total_ref[8][:1, :64]
    store_out.wait()
    store_sg.wait()
    store_back.wait()


WHOLE = pl.BlockSpec(memory_space=pltpu.VMEM)
AWAY = pl.BlockSpec(memory_space=pl.ANY)


def shards(field, cotangent, spectral, skip, bias):
    constants = tuple(jnp.asarray(a) for a in tables())
    shape = lambda dims, dtype: jax.ShapeDtypeStruct(dims, dtype)

    def gather(a):
        return jnp.transpose(a.reshape(C, 4, 32, 128), (0, 2, 1, 3)).reshape(C, 128, 128)

    def spread(a):
        return jnp.transpose(a.reshape(C, 32, 4, 128), (0, 2, 1, 3)).reshape(1, C, 4, N * N)

    grid = pltpu.VMEM((256, N * N), BF)
    turned = pltpu.VMEM((N * N, 256), BF)
    block = pltpu.VMEM((C, 128, 128), BF)
    planes = pltpu.VMEM((8, 512, 256), BF)
    modes = pltpu.VMEM((2048, 128), F32)
    chunks = pltpu.VMEM((2, DEVICES, 16, 128), BF)
    small = lambda count: pltpu.VMEM((count, 8, 128), F32)
    dma = pltpu.SemaphoreType.DMA
    out, back, spectral_grad, skip_grad, bias_grad = pl.pallas_call(
        layer,
        out_shape=(
            shape((C, 128, 128), BF),
            shape((C, 128, 128), BF),
            shape((2, C, C, 256), BF),
            shape((C, C), F32),
            shape((1, C), F32),
        ),
        in_specs=[AWAY, AWAY, AWAY] + [WHOLE] * 12,
        out_specs=[AWAY, AWAY, AWAY, WHOLE, WHOLE],
        scratch_shapes=[
            block, block, pltpu.VMEM((2, C, C, 256), BF), grid, turned, turned, turned,
            pltpu.VMEM((N * N, 256), F32), planes, planes, pltpu.VMEM((256 * 64, 128), F32),
            modes, modes, modes, pltpu.VMEM((256, 256), BF),
            pltpu.VMEM((256, 256), F32), pltpu.VMEM((8, 256), F32),
            small(16), small(16), pltpu.VMEM((8, 128), F32), small(8), small(16),
        ]
        + [chunks] * 6
        + [dma((8,)), dma((8,)), dma((8,)), dma((3,)), dma((3,)), dma((3,)), dma((3,))],
        compiler_params=pltpu.CompilerParams(
            collective_id=1, has_side_effects=True, vmem_limit_bytes=VMEM_LIMIT
        ),
        name="layer",
    )(gather(field), gather(cotangent), spectral, skip, bias.reshape(1, C), *constants)
    return (spread(out), spread(back), spectral_grad, skip_grad, bias_grad[0])


def solution(mesh):
    whole = P("dp", None, "slab", None)
    modes = P(None, None, None, ("slab", "dp"))
    return jax.shard_map(
        shards,
        mesh=mesh,
        in_specs=(whole, whole, modes, P(), P()),
        out_specs=(whole, whole, modes, P(), P()),
        check_vma=False,
    )
```

```python
import functools
import math

import jax
import jax.numpy as jnp
import ml_dtypes
import numpy as np
from jax import lax
from jax.experimental import pallas as pl
from jax.experimental.pallas import tpu as pltpu
from jax.sharding import PartitionSpec as P

N = 64
M = 32
C = 64
DP = 8
SLAB = 16
DEVICES = DP * SLAB
SAMPLES = 8
BF = jnp.bfloat16
F32 = jnp.float32
MESH = pl.DeviceIdType.MESH
VMEM_LIMIT = 56 * 1024 * 1024


def waves():
    phase = np.mod(np.arange(N)[:, None] * (np.arange(M)[None, :] - M // 2), N)
    angle = phase * (2.0 * math.pi / N)
    return np.cos(angle) / 8.0, np.sin(angle) / 8.0


def tables():
    cos, sin = waves()
    pair = np.stack([cos, -sin], 0).reshape(2, N, 4, 2, 4)
    d1 = np.einsum("tzbhl,uv->hbutlvz", pair, np.eye(4)).reshape(256, 256)
    turn = np.stack([np.stack([cos, sin], 0), np.stack([-sin, cos], 0)], 0)
    turn = turn.reshape(2, 2, N, SLAB, 2)
    d2 = np.einsum("stywx,el->xwseytl", turn, np.eye(4)).reshape(256, 512)
    both = np.stack([cos, sin], 0)
    fwd = np.einsum("axk,ef->aekxf", both, np.eye(4)).reshape(256, 256)
    inv = np.einsum("axk,ef->axefk", both, np.eye(4)).reshape(512, 128)
    eye = np.eye(256)
    order = np.eye(256).reshape(64, 4, 256).transpose(1, 0, 2).reshape(256, 256)
    repeat = np.tile(np.eye(64), (4, 1))
    out = (d1, d1.T, d2, d2.T, fwd, inv, eye, order, order.T, repeat)
    return tuple(np.ascontiguousarray(a).astype(ml_dtypes.bfloat16) for a in out)


def dot(a, b):
    return lax.dot_general(a, b, (((1,), (0,)), ((), ())), preferred_element_type=F32)


def dot_nt(a, b):
    return lax.dot_general(a, b, (((1,), (1,)), ((), ())), preferred_element_type=F32)


def low_lanes(shape):
    return lax.broadcasted_iota(jnp.int32, shape, len(shape) - 1) < 64


def swap(v):
    return pltpu.roll(v, 64, v.ndim - 1)


def signed_swap(v, low_sign):
    turned = swap(v)
    low = low_lanes(v.shape)
    return jnp.where(low, turned, -turned) if low_sign > 0 else jnp.where(low, -turned, turned)


def cross(v):
    upper = lax.broadcasted_iota(jnp.int32, v.shape, v.ndim - 2) < 4
    keep = upper == low_lanes(v.shape)
    return jnp.where(keep, v, swap(pltpu.roll(v, 4, v.ndim - 2)))


def rows_apart(w):
    w = w.reshape(32, 2, 8, 128)
    even, odd = w[:, 0], w[:, 1]
    upper = lax.broadcasted_iota(jnp.int32, even.shape, 1) < 4
    first = jnp.where(upper, even, pltpu.roll(odd, 4, 1))
    second = jnp.where(upper, pltpu.roll(even, 4, 1), odd)
    return jnp.concatenate([first.reshape(256, 128), second.reshape(256, 128)], 1)


def rows_together(value):
    first = value[:, :128].reshape(32, 8, 128)
    second = value[:, 128:].reshape(32, 8, 128)
    upper = lax.broadcasted_iota(jnp.int32, first.shape, 1) < 4
    even = jnp.where(upper, first, pltpu.roll(second, 4, 1))
    odd = jnp.where(upper, pltpu.roll(first, 4, 1), second)
    return jnp.stack([even, odd], 1).reshape(64, 8, 128)


def sixteen(index):
    return pl.ds(pl.multiple_of(index * 16, 16), 16)


def stage_y(b_ref, d2_ref, s_ref, half):
    def one(lb, carry):
        f = dot(d2_ref[...], b_ref[half * 4 + lb]).reshape(32, 8, 256)
        chunk = jnp.concatenate([cross(f[:, :, :128]), cross(f[:, :, 128:])], 1).astype(BF)
        s_ref[half, pl.ds(lb * 16, 16)] = chunk[:16]
        s_ref[half, pl.ds(lb * 16 + 64, 16)] = chunk[16:]
        return carry

    lax.fori_loop(0, 4, one, 0, unroll=True)


def unstage_y(r_ref, d2t_ref, h_ref, half):
    def one(lb, carry):
        r = jnp.concatenate(
            [r_ref[half, pl.ds(lb * 16, 16)], r_ref[half, pl.ds(lb * 16 + 64, 16)]], 0
        ).astype(F32)
        rows = jnp.concatenate([cross(r[:, :8]), cross(r[:, 8:])], 2).reshape(256, 256)
        h_ref[half * 4 + lb] = dot(d2t_ref[...], rows.astype(BF)).astype(BF)
        return carry

    lax.fori_loop(0, 4, one, 0, unroll=True)


def store_quad(b_ref, quad, value):
    b_ref[:, pl.ds(pl.multiple_of(quad * 32, 32), 32), :] = value.astype(BF).reshape(8, 32, 256)


def load_quad(h_ref, quad):
    return h_ref[:, pl.ds(pl.multiple_of(quad * 32, 32), 32), :].reshape(256, 256)


def columns(quad):
    return pl.ds(pl.multiple_of(quad * 256, 256), 256)


def line_forward(r_ref, fwd_ref, x_ref, half):
    def one(pair, carry):
        a = r_ref[half, pl.ds(32 * pair, 16)].reshape(256, 128)
        b = r_ref[half, pl.ds(32 * pair + 16, 16)].reshape(256, 128)
        y = dot(fwd_ref[...], jnp.concatenate([a, b], 1))
        for h in range(2):
            lanes = slice(128 * h, 128 * h + 128)
            modes = y[:128, lanes] + signed_swap(y[128:, lanes], 1)
            x_ref[pl.ds(1024 * half + 2 * pair + h, 128, stride=8), :] = modes.astype(BF).astype(F32)
        return carry

    lax.fori_loop(0, 4, one, 0, unroll=True)


def line_inverse(p_ref, inv_ref, s_ref, half):
    def one(pair, carry):
        a = p_ref[pl.ds(1024 * half + 2 * pair, 128, stride=8), :].astype(BF)
        b = p_ref[pl.ds(1024 * half + 2 * pair + 1, 128, stride=8), :].astype(BF)
        y = dot(inv_ref[...], jnp.concatenate([a, b], 1))
        for h in range(2):
            lanes = slice(128 * h, 128 * h + 128)
            lines = y[:256, lanes] + signed_swap(y[256:, lanes], -1)
            s_ref[half, pl.ds(32 * pair + 16 * h, 16)] = lines.astype(BF).reshape(16, 16, 128)
        return carry

    lax.fori_loop(0, 4, one, 0, unroll=True)


PITCH = 72


def four_rows(w_ref, group):
    first = pl.multiple_of(group * (4 * PITCH), 8)
    return jnp.concatenate([w_ref[pl.ds(first + PITCH * m, 64), :] for m in range(4)], 0).astype(BF)


def mix(x_ref, w_ref, p_ref, half):
    row_mode = lax.broadcasted_iota(jnp.int32, (32, 128), 0) // 8
    low = low_lanes((32, 128))

    def one(group, carry):
        x = x_ref[pl.ds(pl.multiple_of(group * 32, 32), 32), :]
        xs = swap(x)
        zero = jnp.zeros_like(x)
        top, bottom = [], []
        for h in range(2):
            even = jnp.logical_and(row_mode == 2 * h, low)
            odd = jnp.logical_and(row_mode == 2 * h + 1, jnp.logical_not(low))
            top.append(jnp.where(even, x, jnp.where(odd, xs, zero)))
            bottom.append(jnp.where(even, xs, jnp.where(odd, x, zero)))
        left = jnp.concatenate(
            [jnp.concatenate(top, 1), jnp.concatenate(bottom, 1)], 0
        ).astype(BF)
        w = four_rows(w_ref, group)
        z = dot(left, w)
        p_ref[pl.ds(pl.multiple_of(group * 32, 32), 32), :] = z[:32] + signed_swap(z[32:], -1)
        return carry

    lax.fori_loop(32 * half, 32 * half + 32, one, 0, unroll=4)


def mix_back(g_ref, w_ref, p_ref, half):
    row_mode = lax.broadcasted_iota(jnp.int32, (32, 128), 0) // 8
    low = low_lanes((32, 128))

    def one(group, carry):
        g = g_ref[pl.ds(pl.multiple_of(group * 32, 32), 32), :]
        left = jnp.concatenate([g, signed_swap(g, 1)], 0).astype(BF)
        w = four_rows(w_ref, group)
        z = dot_nt(left, w)
        z0, z1 = z[:32], z[32:]
        even = row_mode % 2 == 0
        first = row_mode < 2
        a0 = jnp.where(first, z0[:, :128], z0[:, 128:])
        a1 = jnp.where(first, z1[:, :128], z1[:, 128:])
        b0 = jnp.where(even, a0, swap(a0))
        b1 = jnp.where(even, swap(a1), a1)
        p_ref[pl.ds(pl.multiple_of(group * 32, 32), 32), :] = jnp.where(low, b0, b1)
        return carry

    lax.fori_loop(32 * half, 32 * half + 32, one, 0, unroll=4)


ROOT = math.sqrt(2.0 / math.pi)
FACTOR = 1.0 / math.sqrt(SAMPLES * N * N * N)


def turn_weights(raw_ref, eye_ref, w_ref, half):
    lanes = slice(128 * half, 128 * half + 128)

    def one(i, carry):
        plane = jnp.concatenate([raw_ref[0, i, :, lanes], raw_ref[1, i, :, lanes]], 0)
        turned = dot_nt(eye_ref[pl.ds(0, 128), pl.ds(0, 128)], plane)
        w_ref[pl.ds(128 * PITCH * half + i, 128, stride=PITCH), :] = turned
        return carry

    lax.fori_loop(0, 64, one, 0, unroll=4)


def weight_gradient(x_ref, g_ref, eye_ref, out_ref, a_ref):
    lane_mode = (lax.broadcasted_iota(jnp.int32, (64, 256), 1) // 8) % 16

    def one(group, carry):
        rows = pl.ds(pl.multiple_of(group * 128, 128), 128)
        xt = x_ref[rows, :].T
        xt = jnp.concatenate([xt[:64], xt[64:]], 1)
        g = g_ref[rows, :]
        right = jnp.concatenate([g, signed_swap(g, 1)], 0).astype(BF)
        left = jnp.concatenate(
            [jnp.where(lane_mode == m, xt, 0.0) for m in range(16)], 0
        ).astype(BF)
        value = dot(left, right)
        first = pl.multiple_of(group * (16 * PITCH), 8)
        for m in range(16):
            a_ref[pl.ds(first + PITCH * m, 64), :] = value[64 * m : 64 * m + 64]
        return carry

    lax.fori_loop(0, 16, one, 0)

    def turn(i, carry):
        value = a_ref[pl.ds(i, 256, stride=PITCH), :].astype(BF)
        plane = dot_nt(eye_ref[pl.ds(0, 128), pl.ds(0, 128)], value).astype(BF)
        out_ref[0, i] = plane[:64]
        out_ref[1, i] = plane[64:]
        return carry

    lax.fori_loop(0, 64, turn, 0, unroll=4)


def layer(
    field_hbm, cot_hbm, raw_hbm, skip_in, bias_in,
    d1_ref, d1t_ref, d2_ref, d2t_ref, fwd_ref, inv_ref, eye_ref, order_ref, back_order_ref, repeat_ref,
    out_hbm, back_hbm, sg_hbm, skip_ref, line_ref,
    io_ref, cot_ref, raw_ref, v_ref, ct_ref, out_ref, g_ref, vk_ref, h_ref, b_ref, w_ref,
    x_ref, y_ref, p_ref, kron_ref,
    acc_ref, sum_ref, part_ref, slab_ref, half_ref, dp_ref, total_ref,
    s1, s2, r1, r2, r3, r4,
    send_sem, recv_sem, local_sem, load_sem, store_sem, small_send, small_recv,
):
    dp = lax.axis_index("dp")
    slab = lax.axis_index("slab")
    me = dp * SLAB + slab

    def wait_bytes(ref, sem):
        pltpu.make_async_copy(ref, ref, sem).wait()

    column = [slab] + [lax.rem(slab + step, SLAB) for step in range(1, SLAB)]

    def everybody(act):
        def one(turn, carry):
            for step in range(1, SLAB):
                act(lax.rem(dp + turn + step, DP), column[step])
            return carry

        def own(turn, carry):
            act(lax.rem(dp + turn, DP), slab)
            return carry

        lax.fori_loop(0, DP, one, 0)
        lax.fori_loop(1, DP, own, 0, unroll=True)

    barrier = pltpu.get_barrier_semaphore()
    load_field = pltpu.make_async_copy(field_hbm, io_ref, load_sem.at[0])
    load_raw = pltpu.make_async_copy(raw_hbm, raw_ref, load_sem.at[1])
    load_cot = pltpu.make_async_copy(cot_hbm, cot_ref, load_sem.at[2])
    load_field.start()
    load_raw.start()
    load_cot.start()

    everybody(
        lambda row, place: pl.semaphore_signal(
            barrier, inc=1, device_id=(row, place), device_id_type=MESH
        )
    )

    rest = pl.ds(0, DEVICES - 1)

    def send(s_ref, r_ref, phase, half):
        at = 2 * phase + half
        pltpu.make_async_copy(s_ref.at[half, me], r_ref.at[half, me], local_sem.at[at]).start()

        def one(row, place):
            pltpu.make_async_remote_copy(
                src_ref=s_ref.at[half, row * SLAB + place],
                dst_ref=r_ref.at[half, me],
                send_sem=send_sem.at[at],
                recv_sem=recv_sem.at[at],
                device_id=(row, place),
                device_id_type=MESH,
            ).start()

        everybody(one)

    def arrived(s_ref, r_ref, phase, half):
        at = 2 * phase + half
        pltpu.make_async_copy(s_ref.at[half, me], r_ref.at[half, me], local_sem.at[at]).wait()
        wait_bytes(r_ref.at[half, rest], recv_sem.at[at])

    def sent(s_ref, phase):
        for half in range(2):
            wait_bytes(s_ref.at[half, rest], send_sem.at[2 * phase + half])

    wide = dot_nt(dot(repeat_ref[...], skip_in[...]).astype(BF), repeat_ref[...])
    same = (
        lax.broadcasted_iota(jnp.int32, (256, 256), 0) // 64
        == lax.broadcasted_iota(jnp.int32, (256, 256), 1) // 64
    )
    kron_ref[...] = jnp.where(same, wide, 0.0).astype(BF)
    bias = jnp.concatenate([bias_in[...]] * 4, 1)

    load_field.wait()

    def plane_one(index, carry):
        block = io_ref[:, sixteen(index), :].astype(F32)
        for j in range(2):
            v = rows_apart(block[:, 8 * j : 8 * j + 8]).astype(BF)
            v = dot(order_ref[...], v).astype(BF)
            v_ref[:, columns(2 * index + j)] = v
            store_quad(b_ref, 2 * index + j, dot_nt(d1_ref[...], v))
        return carry

    lax.fori_loop(0, 8, plane_one, 0, unroll=2)
    stage_y(b_ref, d2_ref, s1, 0)
    pl.semaphore_wait(barrier, DEVICES - 1)
    send(s1, r1, 0, 0)
    stage_y(b_ref, d2_ref, s1, 1)
    send(s1, r1, 0, 1)
    load_raw.wait()

    for half in range(2):
        turn_weights(raw_ref, eye_ref, w_ref, half)
        arrived(s1, r1, 0, half)
        line_forward(r1, fwd_ref, x_ref, half)
        mix(x_ref, w_ref, p_ref, half)
        line_inverse(p_ref, inv_ref, s2, half)
        send(s2, r2, 1, half)

    load_cot.wait()

    def prepare(index, carry):
        block = cot_ref[:, sixteen(index), :].astype(F32)
        for j in range(2):
            quad = columns(2 * index + j)
            cot = rows_apart(block[:, 8 * j : 8 * j + 8]).astype(BF)
            cot = dot(order_ref[...], cot).astype(BF)
            ct_ref[quad, :] = dot_nt(eye_ref[...], cot).astype(BF)
            vt = dot_nt(eye_ref[...], v_ref[:, quad]).astype(BF)
            vk_ref[quad, :] = dot(vt, kron_ref[...]) + bias
        return carry

    lax.fori_loop(0, 8, prepare, 0, unroll=2)
    for half in range(2):
        arrived(s2, r2, 1, half)
        unstage_y(r2, d2t_ref, h_ref, half)

    def point(index, carry):
        for j in range(2):
            quad = 2 * index + j
            pre = dot(d1t_ref[...], load_quad(h_ref, quad)) + vk_ref[columns(quad), :]
            square = pre * pre
            half = 0.5 + 0.5 * jnp.tanh(pre * (ROOT + (ROOT * 0.044715) * square))
            out = pre * half
            out_ref[columns(quad), :] = out.astype(BF)
            slope = half + out * (1.0 - half) * (2.0 * ROOT + (6.0 * 0.044715 * ROOT) * square)
            g = (ct_ref[columns(quad), :].astype(F32) * slope).astype(BF)
            g_ref[columns(quad), :] = g
            store_quad(b_ref, quad, dot(d1_ref[...], g))
        return carry

    lax.fori_loop(0, 8, point, 0, unroll=2)
    sent(s1, 0)
    for half in range(2):
        stage_y(b_ref, d2_ref, s1, half)
        send(s1, r3, 2, half)

    acc_ref[...] = jnp.zeros_like(acc_ref)
    sum_ref[...] = jnp.zeros_like(sum_ref)

    def outer(quad, carry):
        g = g_ref[columns(quad), :]
        acc_ref[...] += dot(v_ref[:, columns(quad)], g)
        sum_ref[...] += jnp.sum(g.astype(F32).reshape(32, 8, 256), axis=0)
        return carry

    lax.fori_loop(0, 16, outer, 0, unroll=2)
    acc = acc_ref[...]
    low = low_lanes((64, 128))
    a = acc[:64, :128] + acc[128:192, 128:]
    b = acc[64:128, :128] + acc[192:, 128:]
    part_ref[pl.ds(0, 8)] = jnp.where(low, a + swap(b), 0.0).reshape(8, 8, 128)
    line = jnp.sum(sum_ref[...], axis=0, keepdims=True)
    line = line[:, :128] + line[:, 128:]
    line = line + swap(line)
    part_ref[8] = jnp.broadcast_to(line, (8, 128))
    part_ref[pl.ds(9, 7)] = jnp.zeros((7, 8, 128), F32)

    def along_slab(source, target_ref, at, number):
        for step in range(1, SLAB):
            pltpu.make_async_remote_copy(
                src_ref=source(column[step]),
                dst_ref=target_ref.at[at],
                send_sem=small_send.at[number],
                recv_sem=small_recv.at[number],
                device_id=(dp, column[step]),
                device_id_type=MESH,
            ).start()

    few = pl.ds(0, SLAB - 1)
    along_slab(lambda place: part_ref.at[place], slab_ref, slab, 0)

    def turn_out(index, carry):
        both = []
        for j in range(2):
            both.append(rows_together(dot_nt(back_order_ref[...], out_ref[columns(2 * index + j), :])))
        io_ref[:, sixteen(index), :] = jnp.concatenate(both, 1).astype(BF)
        return carry

    lax.fori_loop(0, 8, turn_out, 0, unroll=2)
    store_out = pltpu.make_async_copy(io_ref, out_hbm, store_sem.at[0])
    store_out.start()

    def skip_back(quad, carry):
        vk_ref[columns(quad), :] = dot_nt(g_ref[columns(quad), :], kron_ref[...])
        return carry

    lax.fori_loop(0, 16, skip_back, 0, unroll=2)

    sent(s2, 1)
    for half in range(2):
        arrived(s1, r3, 2, half)
        line_forward(r3, fwd_ref, y_ref, half)
        mix_back(y_ref, w_ref, p_ref, half)
        line_inverse(p_ref, inv_ref, s2, half)
        send(s2, r4, 3, half)

    wait_bytes(part_ref.at[few], small_send.at[0])
    wait_bytes(slab_ref.at[few], small_recv.at[0])
    slab_ref[slab] = part_ref[slab]
    half_ref[...] = jnp.sum(slab_ref[...], axis=0)

    def along_dp(step, carry):
        pltpu.make_async_remote_copy(
            src_ref=half_ref,
            dst_ref=dp_ref.at[dp],
            send_sem=small_send.at[1],
            recv_sem=small_recv.at[1],
            device_id=(lax.rem(dp + step, DP), slab),
            device_id_type=MESH,
        ).start()
        return carry

    lax.fori_loop(1, DP, along_dp, 0)
    weight_gradient(x_ref, y_ref, eye_ref, raw_ref, w_ref)
    store_sg = pltpu.make_async_copy(raw_ref, sg_hbm, store_sem.at[1])
    store_sg.start()

    seven = pl.ds(0, DP - 1)
    wait_bytes(dp_ref.at[seven], small_send.at[1])
    wait_bytes(dp_ref.at[seven], small_recv.at[1])
    dp_ref[dp] = half_ref[...]
    part_ref[slab] = jnp.sum(dp_ref[...], axis=0) * FACTOR
    total_ref[slab] = part_ref[slab]
    along_slab(lambda place: part_ref.at[slab], total_ref, slab, 2)

    for half in range(2):
        arrived(s2, r4, 3, half)
        unstage_y(r4, d2t_ref, h_ref, half)

    def last(index, carry):
        both = []
        for j in range(2):
            quad = 2 * index + j
            value = dot(d1t_ref[...], load_quad(h_ref, quad)) + vk_ref[columns(quad), :]
            both.append(rows_together(dot_nt(back_order_ref[...], value.astype(BF))))
        cot_ref[:, sixteen(index), :] = jnp.concatenate(both, 1).astype(BF)
        return carry

    lax.fori_loop(0, 8, last, 0, unroll=2)
    store_back = pltpu.make_async_copy(cot_ref, back_hbm, store_sem.at[2])
    store_back.start()
    sent(s1, 2)
    sent(s2, 3)
    wait_bytes(part_ref.at[few], small_send.at[2])
    wait_bytes(total_ref.at[few], small_recv.at[2])
    skip_ref[...] = total_ref[pl.ds(0, 8)].reshape(64, 128)[:, :64]
    line_ref[...] = total_ref[8][:1, :64]
    store_out.wait()
    store_sg.wait()
    store_back.wait()


WHOLE = pl.BlockSpec(memory_space=pltpu.VMEM)
AWAY = pl.BlockSpec(memory_space=pl.ANY)


def shards(field, cotangent, spectral, skip, bias):
    constants = tuple(jnp.asarray(a) for a in tables())
    shape = lambda dims, dtype: jax.ShapeDtypeStruct(dims, dtype)

    def gather(a):
        return jnp.transpose(a.reshape(C, 4, 32, 128), (0, 2, 1, 3)).reshape(C, 128, 128)

    def spread(a):
        return jnp.transpose(a.reshape(C, 32, 4, 128), (0, 2, 1, 3)).reshape(1, C, 4, N * N)

    grid = pltpu.VMEM((256, N * N), BF)
    turned = pltpu.VMEM((N * N, 256), BF)
    block = pltpu.VMEM((C, 128, 128), BF)
    planes = pltpu.VMEM((8, 512, 256), BF)
    modes = pltpu.VMEM((2048, 128), F32)
    chunks = pltpu.VMEM((2, DEVICES, 16, 128), BF)
    small = lambda count: pltpu.VMEM((count, 8, 128), F32)
    dma = pltpu.SemaphoreType.DMA
    out, back, spectral_grad, skip_grad, bias_grad = pl.pallas_call(
        layer,
        out_shape=(
            shape((C, 128, 128), BF),
            shape((C, 128, 128), BF),
            shape((2, C, C, 256), BF),
            shape((C, C), F32),
            shape((1, C), F32),
        ),
        in_specs=[AWAY, AWAY, AWAY] + [WHOLE] * 12,
        out_specs=[AWAY, AWAY, AWAY, WHOLE, WHOLE],
        scratch_shapes=[
            block, block, pltpu.VMEM((2, C, C, 256), BF), grid, turned, turned, turned,
            pltpu.VMEM((N * N, 256), F32), planes, planes, pltpu.VMEM((256 * PITCH, 128), F32),
            modes, modes, modes, pltpu.VMEM((256, 256), BF),
            pltpu.VMEM((256, 256), F32), pltpu.VMEM((8, 256), F32),
            small(16), small(16), pltpu.VMEM((8, 128), F32), small(8), small(16),
        ]
        + [chunks] * 6
        + [dma((8,)), dma((8,)), dma((8,)), dma((3,)), dma((3,)), dma((3,)), dma((3,))],
        compiler_params=pltpu.CompilerParams(
            collective_id=1, has_side_effects=True, vmem_limit_bytes=VMEM_LIMIT
        ),
        name="layer",
    )(gather(field), gather(cotangent), spectral, skip, bias.reshape(1, C), *constants)
    return (spread(out), spread(back), spectral_grad, skip_grad, bias_grad[0])


def solution(mesh):
    whole = P("dp", None, "slab", None)
    modes = P(None, None, None, ("slab", "dp"))
    return jax.shard_map(
        shards,
        mesh=mesh,
        in_specs=(whole, whole, modes, P(), P()),
        out_specs=(whole, whole, modes, P(), P()),
        check_vma=False,
    )
```

```python
import functools
import math

import jax
import jax.numpy as jnp
import ml_dtypes
import numpy as np
from jax import lax
from jax.experimental import pallas as pl
from jax.experimental.pallas import tpu as pltpu
from jax.sharding import PartitionSpec as P

N = 64
M = 32
C = 64
DP = 8
SLAB = 16
DEVICES = DP * SLAB
SAMPLES = 8
BF = jnp.bfloat16
F32 = jnp.float32
MESH = pl.DeviceIdType.MESH
VMEM_LIMIT = 56 * 1024 * 1024


def waves():
    phase = np.mod(np.arange(N)[:, None] * (np.arange(M)[None, :] - M // 2), N)
    angle = phase * (2.0 * math.pi / N)
    return np.cos(angle) / 8.0, np.sin(angle) / 8.0


def tables():
    cos, sin = waves()
    pair = np.stack([cos, -sin], 0).reshape(2, N, 4, 2, 4)
    d1 = np.einsum("tzbhl,uv->hbutlvz", pair, np.eye(4)).reshape(256, 256)
    turn = np.stack([np.stack([cos, sin], 0), np.stack([-sin, cos], 0)], 0)
    turn = turn.reshape(2, 2, N, SLAB, 2)
    d2 = np.einsum("stywx,el->xwseytl", turn, np.eye(4)).reshape(256, 512)
    both = np.stack([cos, sin], 0)
    fwd = np.einsum("axk,ef->aekxf", both, np.eye(4)).reshape(256, 256)
    inv = np.einsum("axk,ef->axefk", both, np.eye(4)).reshape(512, 128)
    eye = np.eye(256)
    order = np.eye(256).reshape(64, 4, 256).transpose(1, 0, 2).reshape(256, 256)
    repeat = np.tile(np.eye(64), (4, 1))
    out = (d1, d1.T, d2, d2.T, fwd, inv, eye, order, order.T, repeat)
    return tuple(np.ascontiguousarray(a).astype(ml_dtypes.bfloat16) for a in out)


def dot(a, b):
    return lax.dot_general(a, b, (((1,), (0,)), ((), ())), preferred_element_type=F32)


def dot_nt(a, b):
    return lax.dot_general(a, b, (((1,), (1,)), ((), ())), preferred_element_type=F32)


def low_lanes(shape):
    return lax.broadcasted_iota(jnp.int32, shape, len(shape) - 1) < 64


def swap(v):
    return pltpu.roll(v, 64, v.ndim - 1)


def signed_swap(v, low_sign):
    turned = swap(v)
    low = low_lanes(v.shape)
    return jnp.where(low, turned, -turned) if low_sign > 0 else jnp.where(low, -turned, turned)


def cross(v):
    upper = lax.broadcasted_iota(jnp.int32, v.shape, v.ndim - 2) < 4
    keep = upper == low_lanes(v.shape)
    return jnp.where(keep, v, swap(pltpu.roll(v, 4, v.ndim - 2)))


def rows_apart(w):
    w = w.reshape(32, 2, 8, 128)
    even, odd = w[:, 0], w[:, 1]
    upper = lax.broadcasted_iota(jnp.int32, even.shape, 1) < 4
    first = jnp.where(upper, even, pltpu.roll(odd, 4, 1))
    second = jnp.where(upper, pltpu.roll(even, 4, 1), odd)
    return jnp.concatenate([first.reshape(256, 128), second.reshape(256, 128)], 1)


def rows_together(value):
    first = value[:, :128].reshape(32, 8, 128)
    second = value[:, 128:].reshape(32, 8, 128)
    upper = lax.broadcasted_iota(jnp.int32, first.shape, 1) < 4
    even = jnp.where(upper, first, pltpu.roll(second, 4, 1))
    odd = jnp.where(upper, pltpu.roll(first, 4, 1), second)
    return jnp.stack([even, odd], 1).reshape(64, 8, 128)


def sixteen(index):
    return pl.ds(pl.multiple_of(index * 16, 16), 16)


def stage_y(b_ref, d2_ref, s_ref, half):
    def one(lb, carry):
        f = dot(d2_ref[...], b_ref[half * 4 + lb]).reshape(32, 8, 256)
        chunk = jnp.concatenate([cross(f[:, :, :128]), cross(f[:, :, 128:])], 1).astype(BF)
        s_ref[half, pl.ds(lb * 16, 16)] = chunk[:16]
        s_ref[half, pl.ds(lb * 16 + 64, 16)] = chunk[16:]
        return carry

    lax.fori_loop(0, 4, one, 0, unroll=True)


def unstage_y(r_ref, d2t_ref, h_ref, half):
    def one(lb, carry):
        r = jnp.concatenate(
            [r_ref[half, pl.ds(lb * 16, 16)], r_ref[half, pl.ds(lb * 16 + 64, 16)]], 0
        ).astype(F32)
        rows = jnp.concatenate([cross(r[:, :8]), cross(r[:, 8:])], 2).reshape(256, 256)
        h_ref[half * 4 + lb] = dot(d2t_ref[...], rows.astype(BF)).astype(BF)
        return carry

    lax.fori_loop(0, 4, one, 0, unroll=True)


def store_quad(b_ref, quad, value):
    b_ref[:, pl.ds(pl.multiple_of(quad * 32, 32), 32), :] = value.astype(BF).reshape(8, 32, 256)


def load_quad(h_ref, quad):
    return h_ref[:, pl.ds(pl.multiple_of(quad * 32, 32), 32), :].reshape(256, 256)


def columns(quad):
    return pl.ds(pl.multiple_of(quad * 256, 256), 256)


def line_forward(r_ref, fwd_ref, x_ref, half):
    def one(pair, carry):
        a = r_ref[half, pl.ds(32 * pair, 16)].reshape(256, 128)
        b = r_ref[half, pl.ds(32 * pair + 16, 16)].reshape(256, 128)
        y = dot(fwd_ref[...], jnp.concatenate([a, b], 1))
        for h in range(2):
            lanes = slice(128 * h, 128 * h + 128)
            modes = y[:128, lanes] + signed_swap(y[128:, lanes], 1)
            x_ref[pl.ds(1024 * half + 2 * pair + h, 128, stride=8), :] = modes.astype(BF).astype(F32)
        return carry

    lax.fori_loop(0, 4, one, 0, unroll=True)


def line_inverse(p_ref, inv_ref, s_ref, half):
    def one(pair, carry):
        a = p_ref[pl.ds(1024 * half + 2 * pair, 128, stride=8), :].astype(BF)
        b = p_ref[pl.ds(1024 * half + 2 * pair + 1, 128, stride=8), :].astype(BF)
        y = dot(inv_ref[...], jnp.concatenate([a, b], 1))
        for h in range(2):
            lanes = slice(128 * h, 128 * h + 128)
            lines = y[:256, lanes] + signed_swap(y[256:, lanes], -1)
            s_ref[half, pl.ds(32 * pair + 16 * h, 16)] = lines.astype(BF).reshape(16, 16, 128)
        return carry

    lax.fori_loop(0, 4, one, 0, unroll=True)


PITCH = 72


def four_rows(w_ref, group):
    first = pl.multiple_of(group * (4 * PITCH), 8)
    return jnp.concatenate([w_ref[pl.ds(first + PITCH * m, 64), :] for m in range(4)], 0).astype(BF)


def mix(x_ref, w_ref, p_ref, half):
    row_mode = lax.broadcasted_iota(jnp.int32, (32, 128), 0) // 8
    low = low_lanes((32, 128))

    def spaced(x):
        xs = swap(x)
        zero = jnp.zeros_like(x)
        top, bottom = [], []
        for h in range(2):
            even = jnp.logical_and(row_mode == 2 * h, low)
            odd = jnp.logical_and(row_mode == 2 * h + 1, jnp.logical_not(low))
            top.append(jnp.where(even, x, jnp.where(odd, xs, zero)))
            bottom.append(jnp.where(even, xs, jnp.where(odd, x, zero)))
        return [jnp.concatenate(top, 1), jnp.concatenate(bottom, 1)]

    def one(group, carry):
        rows = [pl.ds(pl.multiple_of(group * 64 + 32 * j, 32), 32) for j in range(2)]
        left = jnp.concatenate(spaced(x_ref[rows[0], :]) + spaced(x_ref[rows[1], :]), 0).astype(BF)
        w = jnp.concatenate([four_rows(w_ref, 2 * group), four_rows(w_ref, 2 * group + 1)], 1)
        z = dot(left, w)
        for j in range(2):
            y = z[64 * j : 64 * j + 64, 128 * j : 128 * j + 128]
            p_ref[rows[j], :] = y[:32] + signed_swap(y[32:], -1)
        return carry

    lax.fori_loop(16 * half, 16 * half + 16, one, 0, unroll=4)


def mix_back(g_ref, w_ref, p_ref, half):
    row_mode = lax.broadcasted_iota(jnp.int32, (32, 128), 0) // 8
    low = low_lanes((32, 128))
    even = row_mode % 2 == 0
    first = row_mode < 2

    def one(group, carry):
        rows = [pl.ds(pl.multiple_of(group * 64 + 32 * j, 32), 32) for j in range(2)]
        left = []
        for j in range(2):
            g = g_ref[rows[j], :]
            both = jnp.concatenate([g, signed_swap(g, 1)], 0)
            none = jnp.zeros_like(both)
            left.append(jnp.concatenate([both, none] if j == 0 else [none, both], 1))
        w = jnp.concatenate([four_rows(w_ref, 2 * group), four_rows(w_ref, 2 * group + 1)], 1)
        z = dot_nt(jnp.concatenate(left, 0).astype(BF), w)
        for j in range(2):
            z0, z1 = z[64 * j : 64 * j + 32], z[64 * j + 32 : 64 * j + 64]
            a0 = jnp.where(first, z0[:, :128], z0[:, 128:])
            a1 = jnp.where(first, z1[:, :128], z1[:, 128:])
            b0 = jnp.where(even, a0, swap(a0))
            b1 = jnp.where(even, swap(a1), a1)
            p_ref[rows[j], :] = jnp.where(low, b0, b1)
        return carry

    lax.fori_loop(16 * half, 16 * half + 16, one, 0, unroll=4)


ROOT = math.sqrt(2.0 / math.pi)
FACTOR = 1.0 / math.sqrt(SAMPLES * N * N * N)


def turn_weights(raw_ref, eye_ref, w_ref, half):
    lanes = slice(128 * half, 128 * half + 128)

    def one(i, carry):
        plane = jnp.concatenate([raw_ref[0, i, :, lanes], raw_ref[1, i, :, lanes]], 0)
        turned = dot_nt(eye_ref[pl.ds(0, 128), pl.ds(0, 128)], plane)
        w_ref[pl.ds(128 * PITCH * half + i, 128, stride=PITCH), :] = turned
        return carry

    lax.fori_loop(0, 64, one, 0, unroll=4)


def weight_gradient(x_ref, g_ref, eye_ref, out_ref, a_ref):
    lane_mode = (lax.broadcasted_iota(jnp.int32, (64, 256), 1) // 8) % 16

    def one(group, carry):
        rows = pl.ds(pl.multiple_of(group * 128, 128), 128)
        xt = x_ref[rows, :].T
        xt = jnp.concatenate([xt[:64], xt[64:]], 1)
        g = g_ref[rows, :]
        right = jnp.concatenate([g, signed_swap(g, 1)], 0).astype(BF)
        left = jnp.concatenate(
            [jnp.where(lane_mode == m, xt, 0.0) for m in range(16)], 0
        ).astype(BF)
        value = dot(left, right)
        first = pl.multiple_of(group * (16 * PITCH), 8)
        for m in range(16):
            a_ref[pl.ds(first + PITCH * m, 64), :] = value[64 * m : 64 * m + 64]
        return carry

    lax.fori_loop(0, 16, one, 0)

    def turn(i, carry):
        value = a_ref[pl.ds(i, 256, stride=PITCH), :].astype(BF)
        plane = dot_nt(eye_ref[pl.ds(0, 128), pl.ds(0, 128)], value).astype(BF)
        out_ref[0, i] = plane[:64]
        out_ref[1, i] = plane[64:]
        return carry

    lax.fori_loop(0, 64, turn, 0, unroll=4)


def spread_map(skip_in, repeat_ref, kron_ref):
    wide = dot_nt(dot(repeat_ref[...], skip_in[...]).astype(BF), repeat_ref[...])
    same = (
        lax.broadcasted_iota(jnp.int32, (256, 256), 0) // 64
        == lax.broadcasted_iota(jnp.int32, (256, 256), 1) // 64
    )
    kron_ref[...] = jnp.where(same, wide, 0.0).astype(BF)


def layer(
    field_hbm, cot_hbm, raw_hbm, skip_in, bias_in,
    d1_ref, d1t_ref, d2_ref, d2t_ref, fwd_ref, inv_ref, eye_ref, order_ref, back_order_ref, repeat_ref,
    out_hbm, sg_hbm, g_hbm, r4, skip_ref, line_ref,
    io_ref, cot_ref, raw_ref, v_ref, ct_ref, out_ref, g_ref, vk_ref, h_ref, b_ref, w_ref,
    x_ref, y_ref, p_ref, kron_ref,
    acc_ref, sum_ref, part_ref, slab_ref, half_ref, dp_ref, total_ref,
    s1, s2, r1, r2, r3,
    send_sem, recv_sem, local_sem, load_sem, store_sem, small_send, small_recv,
):
    dp = lax.axis_index("dp")
    slab = lax.axis_index("slab")
    me = dp * SLAB + slab

    def wait_bytes(ref, sem):
        pltpu.make_async_copy(ref, ref, sem).wait()

    column = [slab] + [lax.rem(slab + step, SLAB) for step in range(1, SLAB)]

    def everybody(act):
        def one(turn, carry):
            for step in range(1, SLAB):
                act(lax.rem(dp + turn + step, DP), column[step])
            return carry

        def own(turn, carry):
            act(lax.rem(dp + turn, DP), slab)
            return carry

        lax.fori_loop(0, DP, one, 0)
        lax.fori_loop(1, DP, own, 0, unroll=True)

    barrier = pltpu.get_barrier_semaphore()
    load_field = pltpu.make_async_copy(field_hbm, io_ref, load_sem.at[0])
    load_raw = pltpu.make_async_copy(raw_hbm, raw_ref, load_sem.at[1])
    load_cot = pltpu.make_async_copy(cot_hbm, cot_ref, load_sem.at[2])
    load_field.start()
    load_raw.start()
    load_cot.start()

    everybody(
        lambda row, place: pl.semaphore_signal(
            barrier, inc=1, device_id=(row, place), device_id_type=MESH
        )
    )

    rest = pl.ds(0, DEVICES - 1)

    def send(s_ref, r_ref, phase, half):
        at = 2 * phase + half
        pltpu.make_async_copy(s_ref.at[half, me], r_ref.at[half, me], local_sem.at[at]).start()

        def one(row, place):
            pltpu.make_async_remote_copy(
                src_ref=s_ref.at[half, row * SLAB + place],
                dst_ref=r_ref.at[half, me],
                send_sem=send_sem.at[at],
                recv_sem=recv_sem.at[at],
                device_id=(row, place),
                device_id_type=MESH,
            ).start()

        everybody(one)

    def arrived(s_ref, r_ref, phase, half):
        at = 2 * phase + half
        pltpu.make_async_copy(s_ref.at[half, me], r_ref.at[half, me], local_sem.at[at]).wait()
        wait_bytes(r_ref.at[half, rest], recv_sem.at[at])

    def sent(s_ref, phase):
        for half in range(2):
            wait_bytes(s_ref.at[half, rest], send_sem.at[2 * phase + half])

    spread_map(skip_in, repeat_ref, kron_ref)
    bias = jnp.concatenate([bias_in[...]] * 4, 1)

    load_field.wait()

    def plane_one(index, carry):
        block = io_ref[:, sixteen(index), :].astype(F32)
        for j in range(2):
            v = rows_apart(block[:, 8 * j : 8 * j + 8]).astype(BF)
            v = dot(order_ref[...], v).astype(BF)
            v_ref[:, columns(2 * index + j)] = v
            store_quad(b_ref, 2 * index + j, dot_nt(d1_ref[...], v))
        return carry

    lax.fori_loop(0, 8, plane_one, 0, unroll=2)
    stage_y(b_ref, d2_ref, s1, 0)
    pl.semaphore_wait(barrier, DEVICES - 1)
    send(s1, r1, 0, 0)
    stage_y(b_ref, d2_ref, s1, 1)
    send(s1, r1, 0, 1)
    load_raw.wait()

    for half in range(2):
        turn_weights(raw_ref, eye_ref, w_ref, half)
        arrived(s1, r1, 0, half)
        line_forward(r1, fwd_ref, x_ref, half)
        mix(x_ref, w_ref, p_ref, half)
        line_inverse(p_ref, inv_ref, s2, half)
        send(s2, r2, 1, half)

    load_cot.wait()

    def prepare(index, carry):
        block = cot_ref[:, sixteen(index), :].astype(F32)
        for j in range(2):
            quad = columns(2 * index + j)
            cot = rows_apart(block[:, 8 * j : 8 * j + 8]).astype(BF)
            cot = dot(order_ref[...], cot).astype(BF)
            ct_ref[quad, :] = dot_nt(eye_ref[...], cot).astype(BF)
            vt = dot_nt(eye_ref[...], v_ref[:, quad]).astype(BF)
            vk_ref[quad, :] = dot(vt, kron_ref[...]) + bias
        return carry

    lax.fori_loop(0, 8, prepare, 0, unroll=2)
    for half in range(2):
        arrived(s2, r2, 1, half)
        unstage_y(r2, d2t_ref, h_ref, half)

    def point(index, carry):
        for j in range(2):
            quad = 2 * index + j
            pre = dot(d1t_ref[...], load_quad(h_ref, quad)) + vk_ref[columns(quad), :]
            square = pre * pre
            half = 0.5 + 0.5 * jnp.tanh(pre * (ROOT + (ROOT * 0.044715) * square))
            out = pre * half
            out_ref[columns(quad), :] = out.astype(BF)
            slope = half + out * (1.0 - half) * (2.0 * ROOT + (6.0 * 0.044715 * ROOT) * square)
            g = (ct_ref[columns(quad), :].astype(F32) * slope).astype(BF)
            g_ref[columns(quad), :] = g
            store_quad(b_ref, quad, dot(d1_ref[...], g))
        return carry

    lax.fori_loop(0, 8, point, 0, unroll=2)
    sent(s1, 0)
    for half in range(2):
        stage_y(b_ref, d2_ref, s1, half)
        send(s1, r3, 2, half)

    store_g = pltpu.make_async_copy(g_ref, g_hbm, store_sem.at[2])
    store_g.start()

    acc_ref[...] = jnp.zeros_like(acc_ref)
    sum_ref[...] = jnp.zeros_like(sum_ref)

    def outer(quad, carry):
        g = g_ref[columns(quad), :]
        acc_ref[...] += dot(v_ref[:, columns(quad)], g)
        sum_ref[...] += jnp.sum(g.astype(F32).reshape(32, 8, 256), axis=0)
        return carry

    lax.fori_loop(0, 16, outer, 0, unroll=2)
    acc = acc_ref[...]
    low = low_lanes((64, 128))
    a = acc[:64, :128] + acc[128:192, 128:]
    b = acc[64:128, :128] + acc[192:, 128:]
    part_ref[pl.ds(0, 8)] = jnp.where(low, a + swap(b), 0.0).reshape(8, 8, 128)
    line = jnp.sum(sum_ref[...], axis=0, keepdims=True)
    line = line[:, :128] + line[:, 128:]
    line = line + swap(line)
    part_ref[8] = jnp.broadcast_to(line, (8, 128))
    part_ref[pl.ds(9, 7)] = jnp.zeros((7, 8, 128), F32)

    def along_slab(source, target_ref, at, number):
        for step in range(1, SLAB):
            pltpu.make_async_remote_copy(
                src_ref=source(column[step]),
                dst_ref=target_ref.at[at],
                send_sem=small_send.at[number],
                recv_sem=small_recv.at[number],
                device_id=(dp, column[step]),
                device_id_type=MESH,
            ).start()

    few = pl.ds(0, SLAB - 1)
    along_slab(lambda place: part_ref.at[place], slab_ref, slab, 0)

    def turn_out(index, carry):
        both = []
        for j in range(2):
            both.append(rows_together(dot_nt(back_order_ref[...], out_ref[columns(2 * index + j), :])))
        io_ref[:, sixteen(index), :] = jnp.concatenate(both, 1).astype(BF)
        return carry

    lax.fori_loop(0, 8, turn_out, 0, unroll=2)
    store_out = pltpu.make_async_copy(io_ref, out_hbm, store_sem.at[0])
    store_out.start()

    sent(s2, 1)
    for half in range(2):
        arrived(s1, r3, 2, half)
        line_forward(r3, fwd_ref, y_ref, half)
        mix_back(y_ref, w_ref, p_ref, half)
        line_inverse(p_ref, inv_ref, s2, half)
        send(s2, r4, 3, half)

    wait_bytes(part_ref.at[few], small_send.at[0])
    wait_bytes(slab_ref.at[few], small_recv.at[0])
    slab_ref[slab] = part_ref[slab]
    half_ref[...] = jnp.sum(slab_ref[...], axis=0)

    def along_dp(step, carry):
        pltpu.make_async_remote_copy(
            src_ref=half_ref,
            dst_ref=dp_ref.at[dp],
            send_sem=small_send.at[1],
            recv_sem=small_recv.at[1],
            device_id=(lax.rem(dp + step, DP), slab),
            device_id_type=MESH,
        ).start()
        return carry

    lax.fori_loop(1, DP, along_dp, 0)
    weight_gradient(x_ref, y_ref, eye_ref, raw_ref, w_ref)
    store_sg = pltpu.make_async_copy(raw_ref, sg_hbm, store_sem.at[1])
    store_sg.start()

    seven = pl.ds(0, DP - 1)
    wait_bytes(dp_ref.at[seven], small_send.at[1])
    wait_bytes(dp_ref.at[seven], small_recv.at[1])
    dp_ref[dp] = half_ref[...]
    part_ref[slab] = jnp.sum(dp_ref[...], axis=0) * FACTOR
    total_ref[slab] = part_ref[slab]
    along_slab(lambda place: part_ref.at[slab], total_ref, slab, 2)

    sent(s1, 2)
    sent(s2, 3)
    wait_bytes(part_ref.at[few], small_send.at[2])
    wait_bytes(total_ref.at[few], small_recv.at[2])
    skip_ref[...] = total_ref[pl.ds(0, 8)].reshape(64, 128)[:, :64]
    line_ref[...] = total_ref[8][:1, :64]
    store_out.wait()
    store_sg.wait()
    store_g.wait()
    for half in range(2):
        arrived(s2, r4, 3, half)


def finish(
    skip_in, skip_part, line_part, repeat_ref, r_hbm, g_hbm, d1t_hbm, d2t_hbm, order_hbm, out_part, sg_part,
    back_hbm, skip_ref, line_ref, out_hbm, sg_hbm,
    r_ref, g_ref, d1t_ref, d2t_ref, back_order_ref, out_ref, sg_ref,
    back_ref, h_ref, kron_ref, load_sem, copy_sem, store_sem,
):
    sources = (r_hbm, d2t_hbm, d1t_hbm, order_hbm, g_hbm, out_part, sg_part)
    targets = (r_ref, d2t_ref, d1t_ref, back_order_ref, g_ref, out_ref, sg_ref)
    loads = [
        pltpu.make_async_copy(source, target, load_sem.at[i])
        for i, (source, target) in enumerate(zip(sources, targets))
    ]
    for load in loads[:5]:
        load.start()
    skip_ref[...] = skip_part[...]
    line_ref[...] = line_part[...]
    spread_map(skip_in, repeat_ref, kron_ref)
    loads[0].wait()
    loads[1].wait()
    for half in range(2):
        unstage_y(r_ref, d2t_ref, h_ref, half)
    for load in loads[2:5]:
        load.wait()
    for load in loads[5:]:
        load.start()

    def last(index, carry):
        both = []
        for j in range(2):
            quad = 2 * index + j
            value = dot(d1t_ref[...], load_quad(h_ref, quad)) + dot_nt(
                g_ref[columns(quad), :], kron_ref[...]
            )
            both.append(rows_together(dot_nt(back_order_ref[...], value.astype(BF))))
        back_ref[:, sixteen(index), :] = jnp.concatenate(both, 1).astype(BF)
        return carry

    def store_back(part):
        rows = pl.ds(32 * part, 32)
        return pltpu.make_async_copy(back_ref.at[:, rows], back_hbm.at[:, rows], store_sem.at[part])

    lax.fori_loop(0, 2, last, 0, unroll=2)
    store_back(0).start()
    lax.fori_loop(2, 4, last, 0, unroll=2)
    store_back(1).start()
    moves = [
        pltpu.make_async_copy(out_ref, out_hbm, copy_sem.at[0]),
        pltpu.make_async_copy(sg_ref, sg_hbm, copy_sem.at[1]),
    ]
    for load, move in zip(loads[5:], moves):
        load.wait()
        move.start()
    lax.fori_loop(4, 6, last, 0, unroll=2)
    store_back(2).start()
    lax.fori_loop(6, 8, last, 0, unroll=2)
    store_back(3).start()
    for move in moves:
        move.wait()
    for part in range(4):
        store_back(part).wait()


WHOLE = pl.BlockSpec(memory_space=pltpu.VMEM)
AWAY = pl.BlockSpec(memory_space=pl.ANY)


def shards(field, cotangent, spectral, skip, bias):
    constants = tuple(jnp.asarray(a) for a in tables())
    d1, d1t, d2, d2t, fwd, inv, eye, order, back_order, repeat = constants
    shape = lambda dims, dtype: jax.ShapeDtypeStruct(dims, dtype)

    def gather(a):
        return jnp.transpose(a.reshape(C, 4, 32, 128), (0, 2, 1, 3)).reshape(C, 128, 128)

    def spread(a):
        return jnp.transpose(a.reshape(C, 32, 4, 128), (0, 2, 1, 3)).reshape(1, C, 4, N * N)

    grid = pltpu.VMEM((256, N * N), BF)
    turned = pltpu.VMEM((N * N, 256), BF)
    block = pltpu.VMEM((C, 128, 128), BF)
    planes = pltpu.VMEM((8, 512, 256), BF)
    modes = pltpu.VMEM((2048, 128), F32)
    chunks = pltpu.VMEM((2, DEVICES, 16, 128), BF)
    square = pltpu.VMEM((256, 256), BF)
    small = lambda count: pltpu.VMEM((count, 8, 128), F32)
    dma = pltpu.SemaphoreType.DMA
    narrow = (shape((C, C), F32), shape((1, C), F32))
    weights = shape((2, C, C, 256), BF)
    cells = shape((C, 128, 128), BF)
    out, spectral_grad, g, r4, skip_grad, bias_grad = pl.pallas_call(
        layer,
        out_shape=(
            cells, weights, shape((N * N, 256), BF), shape((2, DEVICES, 16, 128), BF), *narrow
        ),
        in_specs=[AWAY, AWAY, AWAY] + [WHOLE] * 12,
        out_specs=[AWAY] * 4 + [WHOLE] * 2,
        scratch_shapes=[
            block, block, pltpu.VMEM((2, C, C, 256), BF), grid, turned, turned, turned,
            pltpu.VMEM((N * N, 256), F32), planes, planes, pltpu.VMEM((256 * PITCH, 128), F32),
            modes, modes, modes, pltpu.VMEM((256, 256), BF),
            pltpu.VMEM((256, 256), F32), pltpu.VMEM((8, 256), F32),
            small(16), small(16), pltpu.VMEM((8, 128), F32), small(8), small(16),
        ]
        + [chunks] * 5
        + [dma((8,)), dma((8,)), dma((8,)), dma((3,)), dma((3,)), dma((3,)), dma((3,))],
        compiler_params=pltpu.CompilerParams(
            collective_id=1, has_side_effects=True, vmem_limit_bytes=VMEM_LIMIT
        ),
        name="layer",
    )(gather(field), gather(cotangent), spectral, skip, bias.reshape(1, C), *constants)
    back, skip_grad, bias_grad, out, spectral_grad = pl.pallas_call(
        finish,
        out_shape=(cells, *narrow, cells, weights),
        in_specs=[WHOLE] * 4 + [AWAY] * 7,
        out_specs=[AWAY, WHOLE, WHOLE, AWAY, AWAY],
        scratch_shapes=[
            chunks, turned, square, pltpu.VMEM((512, 256), BF), square, block,
            pltpu.VMEM((2, C, C, 256), BF), block, planes, square,
            dma((7,)), dma((2,)), dma((4,)),
        ],
        compiler_params=pltpu.CompilerParams(vmem_limit_bytes=VMEM_LIMIT),
        name="finish",
    )(skip, skip_grad, bias_grad, repeat, r4, g, d1t, d2t, back_order, out, spectral_grad)
    return (spread(out), spread(back), spectral_grad, skip_grad, bias_grad[0])


def solution(mesh):
    whole = P("dp", None, "slab", None)
    modes = P(None, None, None, ("slab", "dp"))
    return jax.shard_map(
        shards,
        mesh=mesh,
        in_specs=(whole, whole, modes, P(), P()),
        out_specs=(whole, whole, modes, P(), P()),
        check_vma=False,
    )
```

```python
import functools
import math

import jax
import jax.numpy as jnp
import ml_dtypes
import numpy as np
from jax import lax
from jax.experimental import pallas as pl
from jax.experimental.pallas import tpu as pltpu
from jax.sharding import PartitionSpec as P

N = 64
M = 32
C = 64
DP = 8
SLAB = 16
DEVICES = DP * SLAB
SAMPLES = 8
BF = jnp.bfloat16
F32 = jnp.float32
MESH = pl.DeviceIdType.MESH
VMEM_LIMIT = 56 * 1024 * 1024


def waves():
    phase = np.mod(np.arange(N)[:, None] * (np.arange(M)[None, :] - M // 2), N)
    angle = phase * (2.0 * math.pi / N)
    return np.cos(angle) / 8.0, np.sin(angle) / 8.0


def tables():
    cos, sin = waves()
    pair = np.stack([cos, -sin], 0).reshape(2, N, 4, 2, 4)
    d1 = np.einsum("tzbhl,uv->hbutlvz", pair, np.eye(4)).reshape(256, 256)
    turn = np.stack([np.stack([cos, sin], 0), np.stack([-sin, cos], 0)], 0)
    turn = turn.reshape(2, 2, N, SLAB, 2)
    d2 = np.einsum("stywx,el->xwseytl", turn, np.eye(4)).reshape(256, 512)
    both = np.stack([cos, sin], 0)
    fwd = np.einsum("axk,ef->aekxf", both, np.eye(4)).reshape(256, 256)
    inv = np.einsum("axk,ef->axefk", both, np.eye(4)).reshape(512, 128)
    eye = np.eye(256)
    order = np.eye(256).reshape(64, 4, 256).transpose(1, 0, 2).reshape(256, 256)
    repeat = np.tile(np.eye(64), (4, 1))
    out = (d1, d1.T, d2, d2.T, fwd, inv, eye, order, order.T, repeat)
    return tuple(np.ascontiguousarray(a).astype(ml_dtypes.bfloat16) for a in out)


def dot(a, b):
    return lax.dot_general(a, b, (((1,), (0,)), ((), ())), preferred_element_type=F32)


def dot_nt(a, b):
    return lax.dot_general(a, b, (((1,), (1,)), ((), ())), preferred_element_type=F32)


def low_lanes(shape):
    return lax.broadcasted_iota(jnp.int32, shape, len(shape) - 1) < 64


def swap(v):
    return pltpu.roll(v, 64, v.ndim - 1)


def signed_swap(v, low_sign):
    turned = swap(v)
    low = low_lanes(v.shape)
    return jnp.where(low, turned, -turned) if low_sign > 0 else jnp.where(low, -turned, turned)


def cross(v):
    upper = lax.broadcasted_iota(jnp.int32, v.shape, v.ndim - 2) < 4
    keep = upper == low_lanes(v.shape)
    return jnp.where(keep, v, swap(pltpu.roll(v, 4, v.ndim - 2)))


def rows_apart(w):
    w = w.reshape(32, 2, 8, 128)
    even, odd = w[:, 0], w[:, 1]
    upper = lax.broadcasted_iota(jnp.int32, even.shape, 1) < 4
    first = jnp.where(upper, even, pltpu.roll(odd, 4, 1))
    second = jnp.where(upper, pltpu.roll(even, 4, 1), odd)
    return jnp.concatenate([first.reshape(256, 128), second.reshape(256, 128)], 1)


def rows_together(value):
    first = value[:, :128].reshape(32, 8, 128)
    second = value[:, 128:].reshape(32, 8, 128)
    upper = lax.broadcasted_iota(jnp.int32, first.shape, 1) < 4
    even = jnp.where(upper, first, pltpu.roll(second, 4, 1))
    odd = jnp.where(upper, pltpu.roll(first, 4, 1), second)
    return jnp.stack([even, odd], 1).reshape(64, 8, 128)


def sixteen(index):
    return pl.ds(pl.multiple_of(index * 16, 16), 16)


def stage_y(b_ref, d2_ref, s_ref, half):
    def one(lb, carry):
        f = dot(d2_ref[...], b_ref[half * 4 + lb]).reshape(32, 8, 256)
        chunk = jnp.concatenate([cross(f[:, :, :128]), cross(f[:, :, 128:])], 1).astype(BF)
        s_ref[half, pl.ds(lb * 16, 16)] = chunk[:16]
        s_ref[half, pl.ds(lb * 16 + 64, 16)] = chunk[16:]
        return carry

    lax.fori_loop(0, 4, one, 0, unroll=True)


def unstage_y(r_ref, d2t_ref, h_ref, half):
    def one(lb, carry):
        r = jnp.concatenate(
            [r_ref[half, pl.ds(lb * 16, 16)], r_ref[half, pl.ds(lb * 16 + 64, 16)]], 0
        ).astype(F32)
        rows = jnp.concatenate([cross(r[:, :8]), cross(r[:, 8:])], 2).reshape(256, 256)
        h_ref[half * 4 + lb] = dot(d2t_ref[...], rows.astype(BF)).astype(BF)
        return carry

    lax.fori_loop(0, 4, one, 0, unroll=True)


def store_quad(b_ref, quad, value):
    b_ref[:, pl.ds(pl.multiple_of(quad * 32, 32), 32), :] = value.astype(BF).reshape(8, 32, 256)


def load_quad(h_ref, quad):
    return h_ref[:, pl.ds(pl.multiple_of(quad * 32, 32), 32), :].reshape(256, 256)


def columns(quad):
    return pl.ds(pl.multiple_of(quad * 256, 256), 256)


def line_forward(r_ref, fwd_ref, x_ref, half):
    def one(pair, carry):
        a = r_ref[half, pl.ds(32 * pair, 16)].reshape(256, 128)
        b = r_ref[half, pl.ds(32 * pair + 16, 16)].reshape(256, 128)
        y = dot(fwd_ref[...], jnp.concatenate([a, b], 1))
        for h in range(2):
            lanes = slice(128 * h, 128 * h + 128)
            modes = y[:128, lanes] + signed_swap(y[128:, lanes], 1)
            x_ref[pl.ds(1024 * half + 2 * pair + h, 128, stride=8), :] = modes.astype(BF).astype(F32)
        return carry

    lax.fori_loop(0, 4, one, 0, unroll=True)


def line_inverse(p_ref, inv_ref, s_ref, half):
    def one(pair, carry):
        a = p_ref[pl.ds(1024 * half + 2 * pair, 128, stride=8), :].astype(BF)
        b = p_ref[pl.ds(1024 * half + 2 * pair + 1, 128, stride=8), :].astype(BF)
        y = dot(inv_ref[...], jnp.concatenate([a, b], 1))
        for h in range(2):
            lanes = slice(128 * h, 128 * h + 128)
            lines = y[:256, lanes] + signed_swap(y[256:, lanes], -1)
            s_ref[half, pl.ds(32 * pair + 16 * h, 16)] = lines.astype(BF).reshape(16, 16, 128)
        return carry

    lax.fori_loop(0, 4, one, 0, unroll=True)


PITCH = 72


def four_rows(w_ref, group):
    first = pl.multiple_of(group * (4 * PITCH), 8)
    return jnp.concatenate([w_ref[pl.ds(first + PITCH * m, 64), :] for m in range(4)], 0).astype(BF)


def mix(x_ref, w_ref, p_ref, half):
    row_mode = lax.broadcasted_iota(jnp.int32, (32, 128), 0) // 8
    low = low_lanes((32, 128))

    def spaced(x):
        xs = swap(x)
        zero = jnp.zeros_like(x)
        top, bottom = [], []
        for h in range(2):
            even = jnp.logical_and(row_mode == 2 * h, low)
            odd = jnp.logical_and(row_mode == 2 * h + 1, jnp.logical_not(low))
            top.append(jnp.where(even, x, jnp.where(odd, xs, zero)))
            bottom.append(jnp.where(even, xs, jnp.where(odd, x, zero)))
        return [jnp.concatenate(top, 1), jnp.concatenate(bottom, 1)]

    def one(group, carry):
        rows = [pl.ds(pl.multiple_of(group * 64 + 32 * j, 32), 32) for j in range(2)]
        left = jnp.concatenate(spaced(x_ref[rows[0], :]) + spaced(x_ref[rows[1], :]), 0).astype(BF)
        w = jnp.concatenate([four_rows(w_ref, 2 * group), four_rows(w_ref, 2 * group + 1)], 1)
        z = dot(left, w)
        for j in range(2):
            y = z[64 * j : 64 * j + 64, 128 * j : 128 * j + 128]
            p_ref[rows[j], :] = y[:32] + signed_swap(y[32:], -1)
        return carry

    lax.fori_loop(16 * half, 16 * half + 16, one, 0, unroll=4)


def mix_back(g_ref, w_ref, p_ref, half):
    row_mode = lax.broadcasted_iota(jnp.int32, (32, 128), 0) // 8
    low = low_lanes((32, 128))
    even = row_mode % 2 == 0
    first = row_mode < 2

    def one(group, carry):
        rows = [pl.ds(pl.multiple_of(group * 64 + 32 * j, 32), 32) for j in range(2)]
        left = []
        for j in range(2):
            g = g_ref[rows[j], :]
            both = jnp.concatenate([g, signed_swap(g, 1)], 0)
            none = jnp.zeros_like(both)
            left.append(jnp.concatenate([both, none] if j == 0 else [none, both], 1))
        w = jnp.concatenate([four_rows(w_ref, 2 * group), four_rows(w_ref, 2 * group + 1)], 1)
        z = dot_nt(jnp.concatenate(left, 0).astype(BF), w)
        for j in range(2):
            z0, z1 = z[64 * j : 64 * j + 32], z[64 * j + 32 : 64 * j + 64]
            a0 = jnp.where(first, z0[:, :128], z0[:, 128:])
            a1 = jnp.where(first, z1[:, :128], z1[:, 128:])
            b0 = jnp.where(even, a0, swap(a0))
            b1 = jnp.where(even, swap(a1), a1)
            p_ref[rows[j], :] = jnp.where(low, b0, b1)
        return carry

    lax.fori_loop(16 * half, 16 * half + 16, one, 0, unroll=4)


ROOT = math.sqrt(2.0 / math.pi)
FACTOR = 1.0 / math.sqrt(SAMPLES * N * N * N)


def turn_weights(raw_ref, eye_ref, w_ref, half):
    lanes = slice(128 * half, 128 * half + 128)

    def one(i, carry):
        plane = jnp.concatenate([raw_ref[0, i, :, lanes], raw_ref[1, i, :, lanes]], 0)
        turned = dot_nt(eye_ref[pl.ds(0, 128), pl.ds(0, 128)], plane)
        w_ref[pl.ds(128 * PITCH * half + i, 128, stride=PITCH), :] = turned
        return carry

    lax.fori_loop(0, 64, one, 0, unroll=4)


def weight_gradient(x_ref, g_ref, eye_ref, out_ref, a_ref):
    lane_mode = (lax.broadcasted_iota(jnp.int32, (64, 256), 1) // 8) % 16

    def one(group, carry):
        rows = pl.ds(pl.multiple_of(group * 128, 128), 128)
        xt = x_ref[rows, :].T
        xt = jnp.concatenate([xt[:64], xt[64:]], 1)
        g = g_ref[rows, :]
        right = jnp.concatenate([g, signed_swap(g, 1)], 0).astype(BF)
        left = jnp.concatenate(
            [jnp.where(lane_mode == m, xt, 0.0) for m in range(16)], 0
        ).astype(BF)
        value = dot(left, right)
        first = pl.multiple_of(group * (16 * PITCH), 8)
        for m in range(16):
            a_ref[pl.ds(first + PITCH * m, 64), :] = value[64 * m : 64 * m + 64]
        return carry

    lax.fori_loop(0, 16, one, 0)

    def turn(i, carry):
        value = a_ref[pl.ds(i, 256, stride=PITCH), :].astype(BF)
        plane = dot_nt(eye_ref[pl.ds(0, 128), pl.ds(0, 128)], value).astype(BF)
        out_ref[0, i] = plane[:64]
        out_ref[1, i] = plane[64:]
        return carry

    lax.fori_loop(0, 64, turn, 0, unroll=4)


def spread_map(skip_in, repeat_ref, kron_ref):
    wide = dot_nt(dot(repeat_ref[...], skip_in[...]).astype(BF), repeat_ref[...])
    same = (
        lax.broadcasted_iota(jnp.int32, (256, 256), 0) // 64
        == lax.broadcasted_iota(jnp.int32, (256, 256), 1) // 64
    )
    kron_ref[...] = jnp.where(same, wide, 0.0).astype(BF)


def layer(
    field_hbm, cot_hbm, raw_hbm, skip_in, bias_in,
    d1_ref, d1t_ref, d2_ref, d2t_ref, fwd_ref, inv_ref, eye_ref, order_ref, back_order_ref, repeat_ref,
    out_hbm, sg_hbm, g_hbm, r4, skip_ref, line_ref,
    io_ref, cot_ref, raw_ref, v_ref, ct_ref, out_ref, g_ref, vk_ref, h_ref, b_ref, w_ref,
    x_ref, y_ref, p_ref, kron_ref,
    acc_ref, sum_ref, part_ref, slab_ref, half_ref, dp_ref, total_ref,
    s1, s2, r1, r2, r3,
    send_sem, recv_sem, local_sem, load_sem, store_sem, small_send, small_recv,
):
    dp = lax.axis_index("dp")
    slab = lax.axis_index("slab")
    me = dp * SLAB + slab

    def wait_bytes(ref, sem):
        pltpu.make_async_copy(ref, ref, sem).wait()

    column = [slab] + [lax.rem(slab + step, SLAB) for step in range(1, SLAB)]

    def everybody(act):
        def one(turn, carry):
            for step in range(1, SLAB):
                act(lax.rem(dp + turn + step, DP), column[step])
            return carry

        def own(turn, carry):
            act(lax.rem(dp + turn, DP), slab)
            return carry

        lax.fori_loop(0, DP, one, 0)
        lax.fori_loop(1, DP, own, 0, unroll=True)

    barrier = pltpu.get_barrier_semaphore()
    load_field = pltpu.make_async_copy(field_hbm, io_ref, load_sem.at[0])
    load_raw = pltpu.make_async_copy(raw_hbm, raw_ref, load_sem.at[1])
    load_cot = pltpu.make_async_copy(cot_hbm, cot_ref, load_sem.at[2])
    load_field.start()
    load_raw.start()
    load_cot.start()

    everybody(
        lambda row, place: pl.semaphore_signal(
            barrier, inc=1, device_id=(row, place), device_id_type=MESH
        )
    )

    rest = pl.ds(0, DEVICES - 1)

    def send(s_ref, r_ref, phase, half):
        at = 2 * phase + half
        pltpu.make_async_copy(s_ref.at[half, me], r_ref.at[half, me], local_sem.at[at]).start()

        def one(row, place):
            pltpu.make_async_remote_copy(
                src_ref=s_ref.at[half, row * SLAB + place],
                dst_ref=r_ref.at[half, me],
                send_sem=send_sem.at[at],
                recv_sem=recv_sem.at[at],
                device_id=(row, place),
                device_id_type=MESH,
            ).start()

        everybody(one)

    def arrived(s_ref, r_ref, phase, half):
        at = 2 * phase + half
        pltpu.make_async_copy(s_ref.at[half, me], r_ref.at[half, me], local_sem.at[at]).wait()
        wait_bytes(r_ref.at[half, rest], recv_sem.at[at])

    def sent(s_ref, phase):
        for half in range(2):
            wait_bytes(s_ref.at[half, rest], send_sem.at[2 * phase + half])

    spread_map(skip_in, repeat_ref, kron_ref)
    bias = jnp.concatenate([bias_in[...]] * 4, 1)

    load_field.wait()

    def plane_one(index, carry):
        block = io_ref[:, sixteen(index), :].astype(F32)
        for j in range(2):
            v = rows_apart(block[:, 8 * j : 8 * j + 8]).astype(BF)
            v = dot(order_ref[...], v).astype(BF)
            v_ref[:, columns(2 * index + j)] = v
            store_quad(b_ref, 2 * index + j, dot_nt(d1_ref[...], v))
        return carry

    lax.fori_loop(0, 8, plane_one, 0, unroll=2)
    stage_y(b_ref, d2_ref, s1, 0)
    pl.semaphore_wait(barrier, DEVICES - 1)
    send(s1, r1, 0, 0)
    stage_y(b_ref, d2_ref, s1, 1)
    send(s1, r1, 0, 1)
    load_raw.wait()

    turn_weights(raw_ref, eye_ref, w_ref, 0)
    turn_weights(raw_ref, eye_ref, w_ref, 1)
    for half in range(2):
        arrived(s1, r1, 0, half)
        line_forward(r1, fwd_ref, x_ref, half)
        mix(x_ref, w_ref, p_ref, half)
        line_inverse(p_ref, inv_ref, s2, half)
        send(s2, r2, 1, half)

    load_cot.wait()

    def prepare(index, carry):
        block = cot_ref[:, sixteen(index), :].astype(F32)
        for j in range(2):
            quad = columns(2 * index + j)
            cot = rows_apart(block[:, 8 * j : 8 * j + 8]).astype(BF)
            cot = dot(order_ref[...], cot).astype(BF)
            ct_ref[quad, :] = dot_nt(eye_ref[...], cot).astype(BF)
            vt = dot_nt(eye_ref[...], v_ref[:, quad]).astype(BF)
            vk_ref[quad, :] = dot(vt, kron_ref[...]) + bias
        return carry

    lax.fori_loop(0, 8, prepare, 0, unroll=2)
    for half in range(2):
        arrived(s2, r2, 1, half)
        unstage_y(r2, d2t_ref, h_ref, half)

    def point(index, carry):
        for j in range(2):
            quad = 2 * index + j
            pre = dot(d1t_ref[...], load_quad(h_ref, quad)) + vk_ref[columns(quad), :]
            square = pre * pre
            half = 0.5 + 0.5 * jnp.tanh(pre * (ROOT + (ROOT * 0.044715) * square))
            out = pre * half
            out_ref[columns(quad), :] = out.astype(BF)
            slope = half + out * (1.0 - half) * (2.0 * ROOT + (6.0 * 0.044715 * ROOT) * square)
            g = (ct_ref[columns(quad), :].astype(F32) * slope).astype(BF)
            g_ref[columns(quad), :] = g
            store_quad(b_ref, quad, dot(d1_ref[...], g))
        return carry

    lax.fori_loop(0, 8, point, 0, unroll=4)
    sent(s1, 0)
    for half in range(2):
        stage_y(b_ref, d2_ref, s1, half)
        send(s1, r3, 2, half)

    store_g = pltpu.make_async_copy(g_ref, g_hbm, store_sem.at[2])
    store_g.start()

    acc_ref[...] = jnp.zeros_like(acc_ref)
    sum_ref[...] = jnp.zeros_like(sum_ref)

    def outer(quad, carry):
        g = g_ref[columns(quad), :]
        acc_ref[...] += dot(v_ref[:, columns(quad)], g)
        sum_ref[...] += jnp.sum(g.astype(F32).reshape(32, 8, 256), axis=0)
        return carry

    lax.fori_loop(0, 16, outer, 0, unroll=2)
    acc = acc_ref[...]
    low = low_lanes((64, 128))
    a = acc[:64, :128] + acc[128:192, 128:]
    b = acc[64:128, :128] + acc[192:, 128:]
    part_ref[pl.ds(0, 8)] = jnp.where(low, a + swap(b), 0.0).reshape(8, 8, 128)
    line = jnp.sum(sum_ref[...], axis=0, keepdims=True)
    line = line[:, :128] + line[:, 128:]
    line = line + swap(line)
    part_ref[8] = jnp.broadcast_to(line, (8, 128))
    part_ref[pl.ds(9, 7)] = jnp.zeros((7, 8, 128), F32)

    def along_slab(source, target_ref, at, number):
        for step in range(1, SLAB):
            pltpu.make_async_remote_copy(
                src_ref=source(column[step]),
                dst_ref=target_ref.at[at],
                send_sem=small_send.at[number],
                recv_sem=small_recv.at[number],
                device_id=(dp, column[step]),
                device_id_type=MESH,
            ).start()

    few = pl.ds(0, SLAB - 1)
    along_slab(lambda place: part_ref.at[place], slab_ref, slab, 0)

    def turn_out(index, carry):
        both = []
        for j in range(2):
            both.append(rows_together(dot_nt(back_order_ref[...], out_ref[columns(2 * index + j), :])))
        io_ref[:, sixteen(index), :] = jnp.concatenate(both, 1).astype(BF)
        return carry

    lax.fori_loop(0, 8, turn_out, 0, unroll=2)
    store_out = pltpu.make_async_copy(io_ref, out_hbm, store_sem.at[0])
    store_out.start()

    sent(s2, 1)
    for half in range(2):
        arrived(s1, r3, 2, half)
        line_forward(r3, fwd_ref, y_ref, half)
        mix_back(y_ref, w_ref, p_ref, half)
        line_inverse(p_ref, inv_ref, s2, half)
        send(s2, r4, 3, half)

    wait_bytes(part_ref.at[few], small_send.at[0])
    wait_bytes(slab_ref.at[few], small_recv.at[0])
    slab_ref[slab] = part_ref[slab]
    half_ref[...] = jnp.sum(slab_ref[...], axis=0)

    def along_dp(step, carry):
        pltpu.make_async_remote_copy(
            src_ref=half_ref,
            dst_ref=dp_ref.at[dp],
            send_sem=small_send.at[1],
            recv_sem=small_recv.at[1],
            device_id=(lax.rem(dp + step, DP), slab),
            device_id_type=MESH,
        ).start()
        return carry

    lax.fori_loop(1, DP, along_dp, 0)
    weight_gradient(x_ref, y_ref, eye_ref, raw_ref, w_ref)
    store_sg = pltpu.make_async_copy(raw_ref, sg_hbm, store_sem.at[1])
    store_sg.start()

    seven = pl.ds(0, DP - 1)
    wait_bytes(dp_ref.at[seven], small_send.at[1])
    wait_bytes(dp_ref.at[seven], small_recv.at[1])
    dp_ref[dp] = half_ref[...]
    part_ref[slab] = jnp.sum(dp_ref[...], axis=0) * FACTOR
    total_ref[slab] = part_ref[slab]
    along_slab(lambda place: part_ref.at[slab], total_ref, slab, 2)

    sent(s1, 2)
    sent(s2, 3)
    wait_bytes(part_ref.at[few], small_send.at[2])
    wait_bytes(total_ref.at[few], small_recv.at[2])
    skip_ref[...] = total_ref[pl.ds(0, 8)].reshape(64, 128)[:, :64]
    line_ref[...] = total_ref[8][:1, :64]
    store_out.wait()
    store_sg.wait()
    store_g.wait()
    for half in range(2):
        arrived(s2, r4, 3, half)


def finish(
    skip_in, skip_part, line_part, repeat_ref, r_hbm, g_hbm, d1t_hbm, d2t_hbm, order_hbm, out_part, sg_part,
    back_hbm, skip_ref, line_ref, out_hbm, sg_hbm,
    r_ref, g_ref, d1t_ref, d2t_ref, back_order_ref, out_ref, sg_ref,
    back_ref, h_ref, kron_ref, load_sem, copy_sem, store_sem,
):
    sources = (r_hbm, d2t_hbm, d1t_hbm, order_hbm, g_hbm, out_part, sg_part)
    targets = (r_ref, d2t_ref, d1t_ref, back_order_ref, g_ref, out_ref, sg_ref)
    loads = [
        pltpu.make_async_copy(source, target, load_sem.at[i])
        for i, (source, target) in enumerate(zip(sources, targets))
    ]
    for load in loads[:5]:
        load.start()
    skip_ref[...] = skip_part[...]
    line_ref[...] = line_part[...]
    spread_map(skip_in, repeat_ref, kron_ref)
    loads[0].wait()
    loads[1].wait()
    for half in range(2):
        unstage_y(r_ref, d2t_ref, h_ref, half)
    for load in loads[2:5]:
        load.wait()
    for load in loads[5:]:
        load.start()

    def last(index, carry):
        both = []
        for j in range(2):
            quad = 2 * index + j
            value = dot(d1t_ref[...], load_quad(h_ref, quad)) + dot_nt(
                g_ref[columns(quad), :], kron_ref[...]
            )
            both.append(rows_together(dot_nt(back_order_ref[...], value.astype(BF))))
        back_ref[:, sixteen(index), :] = jnp.concatenate(both, 1).astype(BF)
        return carry

    def store_back(part):
        rows = pl.ds(32 * part, 32)
        return pltpu.make_async_copy(back_ref.at[:, rows], back_hbm.at[:, rows], store_sem.at[part])

    lax.fori_loop(0, 2, last, 0, unroll=2)
    store_back(0).start()
    lax.fori_loop(2, 4, last, 0, unroll=2)
    store_back(1).start()
    moves = [
        pltpu.make_async_copy(out_ref, out_hbm, copy_sem.at[0]),
        pltpu.make_async_copy(sg_ref, sg_hbm, copy_sem.at[1]),
    ]
    for load, move in zip(loads[5:], moves):
        load.wait()
        move.start()
    lax.fori_loop(4, 6, last, 0, unroll=2)
    store_back(2).start()
    lax.fori_loop(6, 8, last, 0, unroll=2)
    store_back(3).start()
    for move in moves:
        move.wait()
    for part in range(4):
        store_back(part).wait()


WHOLE = pl.BlockSpec(memory_space=pltpu.VMEM)
AWAY = pl.BlockSpec(memory_space=pl.ANY)


def shards(field, cotangent, spectral, skip, bias):
    constants = tuple(jnp.asarray(a) for a in tables())
    d1, d1t, d2, d2t, fwd, inv, eye, order, back_order, repeat = constants
    shape = lambda dims, dtype: jax.ShapeDtypeStruct(dims, dtype)

    def gather(a):
        return jnp.transpose(a.reshape(C, 4, 32, 128), (0, 2, 1, 3)).reshape(C, 128, 128)

    def spread(a):
        return jnp.transpose(a.reshape(C, 32, 4, 128), (0, 2, 1, 3)).reshape(1, C, 4, N * N)

    grid = pltpu.VMEM((256, N * N), BF)
    turned = pltpu.VMEM((N * N, 256), BF)
    block = pltpu.VMEM((C, 128, 128), BF)
    planes = pltpu.VMEM((8, 512, 256), BF)
    modes = pltpu.VMEM((2048, 128), F32)
    chunks = pltpu.VMEM((2, DEVICES, 16, 128), BF)
    square = pltpu.VMEM((256, 256), BF)
    small = lambda count: pltpu.VMEM((count, 8, 128), F32)
    dma = pltpu.SemaphoreType.DMA
    narrow = (shape((C, C), F32), shape((1, C), F32))
    weights = shape((2, C, C, 256), BF)
    cells = shape((C, 128, 128), BF)
    out, spectral_grad, g, r4, skip_grad, bias_grad = pl.pallas_call(
        layer,
        out_shape=(
            cells, weights, shape((N * N, 256), BF), shape((2, DEVICES, 16, 128), BF), *narrow
        ),
        in_specs=[AWAY, AWAY, AWAY] + [WHOLE] * 12,
        out_specs=[AWAY] * 4 + [WHOLE] * 2,
        scratch_shapes=[
            block, block, pltpu.VMEM((2, C, C, 256), BF), grid, turned, turned, turned,
            pltpu.VMEM((N * N, 256), F32), planes, planes, pltpu.VMEM((256 * PITCH, 128), F32),
            modes, modes, modes, pltpu.VMEM((256, 256), BF),
            pltpu.VMEM((256, 256), F32), pltpu.VMEM((8, 256), F32),
            small(16), small(16), pltpu.VMEM((8, 128), F32), small(8), small(16),
        ]
        + [chunks] * 5
        + [dma((8,)), dma((8,)), dma((8,)), dma((3,)), dma((3,)), dma((3,)), dma((3,))],
        compiler_params=pltpu.CompilerParams(
            collective_id=1, has_side_effects=True, vmem_limit_bytes=VMEM_LIMIT
        ),
        name="layer",
    )(gather(field), gather(cotangent), spectral, skip, bias.reshape(1, C), *constants)
    back, skip_grad, bias_grad, out, spectral_grad = pl.pallas_call(
        finish,
        out_shape=(cells, *narrow, cells, weights),
        in_specs=[WHOLE] * 4 + [AWAY] * 7,
        out_specs=[AWAY, WHOLE, WHOLE, AWAY, AWAY],
        scratch_shapes=[
            chunks, turned, square, pltpu.VMEM((512, 256), BF), square, block,
            pltpu.VMEM((2, C, C, 256), BF), block, planes, square,
            dma((7,)), dma((2,)), dma((4,)),
        ],
        compiler_params=pltpu.CompilerParams(vmem_limit_bytes=VMEM_LIMIT),
        name="finish",
    )(skip, skip_grad, bias_grad, repeat, r4, g, d1t, d2t, back_order, out, spectral_grad)
    return (spread(out), spread(back), spectral_grad, skip_grad, bias_grad[0])


def solution(mesh):
    whole = P("dp", None, "slab", None)
    modes = P(None, None, None, ("slab", "dp"))
    return jax.shard_map(
        shards,
        mesh=mesh,
        in_specs=(whole, whole, modes, P(), P()),
        out_specs=(whole, whole, modes, P(), P()),
        check_vma=False,
    )
```

```python
import functools
import math

import jax
import jax.numpy as jnp
import ml_dtypes
import numpy as np
from jax import lax
from jax.experimental import pallas as pl
from jax.experimental.pallas import tpu as pltpu
from jax.sharding import PartitionSpec as P

N = 64
M = 32
C = 64
DP = 8
SLAB = 16
DEVICES = DP * SLAB
SAMPLES = 8
BF = jnp.bfloat16
F32 = jnp.float32
MESH = pl.DeviceIdType.MESH
VMEM_LIMIT = 56 * 1024 * 1024


def waves():
    phase = np.mod(np.arange(N)[:, None] * (np.arange(M)[None, :] - M // 2), N)
    angle = phase * (2.0 * math.pi / N)
    return np.cos(angle) / 8.0, np.sin(angle) / 8.0


def tables():
    cos, sin = waves()
    pair = np.stack([cos, -sin], 0).reshape(2, N, 4, 2, 4)
    d1 = np.einsum("tzbhl,uv->hbutlvz", pair, np.eye(4)).reshape(256, 256)
    turn = np.stack([np.stack([cos, sin], 0), np.stack([-sin, cos], 0)], 0)
    turn = turn.reshape(2, 2, N, SLAB, 2)
    d2 = np.einsum("stywx,el->xwseytl", turn, np.eye(4)).reshape(256, 512)
    both = np.stack([cos, sin], 0)
    fwd = np.einsum("axk,ef->aekxf", both, np.eye(4)).reshape(256, 256)
    inv = np.einsum("axk,ef->axefk", both, np.eye(4)).reshape(512, 128)
    eye = np.eye(256)
    order = np.eye(256).reshape(64, 4, 256).transpose(1, 0, 2).reshape(256, 256)
    repeat = np.tile(np.eye(64), (4, 1))
    out = (d1, d1.T, d2, d2.T, fwd, inv, eye, order, order.T, repeat)
    return tuple(np.ascontiguousarray(a).astype(ml_dtypes.bfloat16) for a in out)


def dot(a, b):
    return lax.dot_general(a, b, (((1,), (0,)), ((), ())), preferred_element_type=F32)


def dot_nt(a, b):
    return lax.dot_general(a, b, (((1,), (1,)), ((), ())), preferred_element_type=F32)


def low_lanes(shape):
    return lax.broadcasted_iota(jnp.int32, shape, len(shape) - 1) < 64


def swap(v):
    return pltpu.roll(v, 64, v.ndim - 1)


def signed_swap(v, low_sign):
    turned = swap(v)
    low = low_lanes(v.shape)
    return jnp.where(low, turned, -turned) if low_sign > 0 else jnp.where(low, -turned, turned)


def cross(v):
    upper = lax.broadcasted_iota(jnp.int32, v.shape, v.ndim - 2) < 4
    keep = upper == low_lanes(v.shape)
    return jnp.where(keep, v, swap(pltpu.roll(v, 4, v.ndim - 2)))


def rows_apart(w):
    w = w.reshape(32, 2, 8, 128)
    even, odd = w[:, 0], w[:, 1]
    upper = lax.broadcasted_iota(jnp.int32, even.shape, 1) < 4
    first = jnp.where(upper, even, pltpu.roll(odd, 4, 1))
    second = jnp.where(upper, pltpu.roll(even, 4, 1), odd)
    return jnp.concatenate([first.reshape(256, 128), second.reshape(256, 128)], 1)


def rows_together(value):
    first = value[:, :128].reshape(32, 8, 128)
    second = value[:, 128:].reshape(32, 8, 128)
    upper = lax.broadcasted_iota(jnp.int32, first.shape, 1) < 4
    even = jnp.where(upper, first, pltpu.roll(second, 4, 1))
    odd = jnp.where(upper, pltpu.roll(first, 4, 1), second)
    return jnp.stack([even, odd], 1).reshape(64, 8, 128)


def sixteen(index):
    return pl.ds(pl.multiple_of(index * 16, 16), 16)


def stage_y(b_ref, d2_ref, s_ref, half):
    def one(lb, carry):
        f = dot(d2_ref[...], b_ref[half * 4 + lb]).reshape(32, 8, 256)
        chunk = jnp.concatenate([cross(f[:, :, :128]), cross(f[:, :, 128:])], 1).astype(BF)
        s_ref[half, pl.ds(lb * 16, 16)] = chunk[:16]
        s_ref[half, pl.ds(lb * 16 + 64, 16)] = chunk[16:]
        return carry

    lax.fori_loop(0, 4, one, 0, unroll=True)


def unstage_y(r_ref, d2t_ref, h_ref, half):
    def one(lb, carry):
        r = jnp.concatenate(
            [r_ref[half, pl.ds(lb * 16, 16)], r_ref[half, pl.ds(lb * 16 + 64, 16)]], 0
        ).astype(F32)
        rows = jnp.concatenate([cross(r[:, :8]), cross(r[:, 8:])], 2).reshape(256, 256)
        h_ref[half * 4 + lb] = dot(d2t_ref[...], rows.astype(BF)).astype(BF)
        return carry

    lax.fori_loop(0, 4, one, 0, unroll=True)


def store_quad(b_ref, quad, value):
    b_ref[:, pl.ds(pl.multiple_of(quad * 32, 32), 32), :] = value.astype(BF).reshape(8, 32, 256)


def load_quad(h_ref, quad):
    return h_ref[:, pl.ds(pl.multiple_of(quad * 32, 32), 32), :].reshape(256, 256)


def columns(quad):
    return pl.ds(pl.multiple_of(quad * 256, 256), 256)


def line_forward(r_ref, fwd_ref, x_ref, half):
    def one(pair, carry):
        a = r_ref[half, pl.ds(32 * pair, 16)].reshape(256, 128)
        b = r_ref[half, pl.ds(32 * pair + 16, 16)].reshape(256, 128)
        y = dot(fwd_ref[...], jnp.concatenate([a, b], 1))
        for h in range(2):
            lanes = slice(128 * h, 128 * h + 128)
            modes = y[:128, lanes] + signed_swap(y[128:, lanes], 1)
            x_ref[pl.ds(1024 * half + 2 * pair + h, 128, stride=8), :] = modes.astype(BF).astype(F32)
        return carry

    lax.fori_loop(0, 4, one, 0, unroll=True)


def line_inverse(p_ref, inv_ref, s_ref, half):
    def one(pair, carry):
        a = p_ref[pl.ds(1024 * half + 2 * pair, 128, stride=8), :].astype(BF)
        b = p_ref[pl.ds(1024 * half + 2 * pair + 1, 128, stride=8), :].astype(BF)
        y = dot(inv_ref[...], jnp.concatenate([a, b], 1))
        for h in range(2):
            lanes = slice(128 * h, 128 * h + 128)
            lines = y[:256, lanes] + signed_swap(y[256:, lanes], -1)
            s_ref[half, pl.ds(32 * pair + 16 * h, 16)] = lines.astype(BF).reshape(16, 16, 128)
        return carry

    lax.fori_loop(0, 4, one, 0, unroll=True)


PITCH = 72


def four_rows(w_ref, group):
    first = pl.multiple_of(group * (4 * PITCH), 8)
    return jnp.concatenate([w_ref[pl.ds(first + PITCH * m, 64), :] for m in range(4)], 0).astype(BF)


def mix(x_ref, w_ref, p_ref, half):
    row_mode = lax.broadcasted_iota(jnp.int32, (32, 128), 0) // 8
    low = low_lanes((32, 128))

    def spaced(x):
        xs = swap(x)
        zero = jnp.zeros_like(x)
        top, bottom = [], []
        for h in range(2):
            even = jnp.logical_and(row_mode == 2 * h, low)
            odd = jnp.logical_and(row_mode == 2 * h + 1, jnp.logical_not(low))
            top.append(jnp.where(even, x, jnp.where(odd, xs, zero)))
            bottom.append(jnp.where(even, xs, jnp.where(odd, x, zero)))
        return [jnp.concatenate(top, 1), jnp.concatenate(bottom, 1)]

    def one(group, carry):
        rows = [pl.ds(pl.multiple_of(group * 64 + 32 * j, 32), 32) for j in range(2)]
        left = jnp.concatenate(spaced(x_ref[rows[0], :]) + spaced(x_ref[rows[1], :]), 0).astype(BF)
        w = jnp.concatenate([four_rows(w_ref, 2 * group), four_rows(w_ref, 2 * group + 1)], 1)
        z = dot(left, w)
        for j in range(2):
            y = z[64 * j : 64 * j + 64, 128 * j : 128 * j + 128]
            p_ref[rows[j], :] = y[:32] + signed_swap(y[32:], -1)
        return carry

    lax.fori_loop(16 * half, 16 * half + 16, one, 0, unroll=8)


def mix_back(g_ref, w_ref, p_ref, half):
    row_mode = lax.broadcasted_iota(jnp.int32, (32, 128), 0) // 8
    low = low_lanes((32, 128))
    even = row_mode % 2 == 0
    first = row_mode < 2

    def one(group, carry):
        rows = [pl.ds(pl.multiple_of(group * 64 + 32 * j, 32), 32) for j in range(2)]
        left = []
        for j in range(2):
            g = g_ref[rows[j], :]
            both = jnp.concatenate([g, signed_swap(g, 1)], 0)
            none = jnp.zeros_like(both)
            left.append(jnp.concatenate([both, none] if j == 0 else [none, both], 1))
        w = jnp.concatenate([four_rows(w_ref, 2 * group), four_rows(w_ref, 2 * group + 1)], 1)
        z = dot_nt(jnp.concatenate(left, 0).astype(BF), w)
        for j in range(2):
            z0, z1 = z[64 * j : 64 * j + 32], z[64 * j + 32 : 64 * j + 64]
            a0 = jnp.where(first, z0[:, :128], z0[:, 128:])
            a1 = jnp.where(first, z1[:, :128], z1[:, 128:])
            b0 = jnp.where(even, a0, swap(a0))
            b1 = jnp.where(even, swap(a1), a1)
            p_ref[rows[j], :] = jnp.where(low, b0, b1)
        return carry

    lax.fori_loop(16 * half, 16 * half + 16, one, 0, unroll=8)


ROOT = math.sqrt(2.0 / math.pi)
FACTOR = 1.0 / math.sqrt(SAMPLES * N * N * N)


def turn_weights(raw_ref, eye_ref, w_ref, half):
    lanes = slice(128 * half, 128 * half + 128)

    def one(i, carry):
        plane = jnp.concatenate([raw_ref[0, i, :, lanes], raw_ref[1, i, :, lanes]], 0)
        turned = dot_nt(eye_ref[pl.ds(0, 128), pl.ds(0, 128)], plane)
        w_ref[pl.ds(128 * PITCH * half + i, 128, stride=PITCH), :] = turned
        return carry

    lax.fori_loop(0, 64, one, 0, unroll=4)


def weight_gradient(x_ref, g_ref, eye_ref, out_ref, a_ref):
    lane_mode = (lax.broadcasted_iota(jnp.int32, (64, 256), 1) // 8) % 16

    def one(group, carry):
        rows = pl.ds(pl.multiple_of(group * 128, 128), 128)
        xt = x_ref[rows, :].T
        xt = jnp.concatenate([xt[:64], xt[64:]], 1)
        g = g_ref[rows, :]
        right = jnp.concatenate([g, signed_swap(g, 1)], 0).astype(BF)
        left = jnp.concatenate(
            [jnp.where(lane_mode == m, xt, 0.0) for m in range(16)], 0
        ).astype(BF)
        value = dot(left, right)
        first = pl.multiple_of(group * (16 * PITCH), 8)
        for m in range(16):
            a_ref[pl.ds(first + PITCH * m, 64), :] = value[64 * m : 64 * m + 64]
        return carry

    lax.fori_loop(0, 16, one, 0, unroll=2)

    def turn(i, carry):
        value = a_ref[pl.ds(i, 256, stride=PITCH), :].astype(BF)
        plane = dot_nt(eye_ref[pl.ds(0, 128), pl.ds(0, 128)], value).astype(BF)
        out_ref[0, i] = plane[:64]
        out_ref[1, i] = plane[64:]
        return carry

    lax.fori_loop(0, 64, turn, 0, unroll=4)


def spread_map(skip_in, repeat_ref, kron_ref):
    wide = dot_nt(dot(repeat_ref[...], skip_in[...]).astype(BF), repeat_ref[...])
    same = (
        lax.broadcasted_iota(jnp.int32, (256, 256), 0) // 64
        == lax.broadcasted_iota(jnp.int32, (256, 256), 1) // 64
    )
    kron_ref[...] = jnp.where(same, wide, 0.0).astype(BF)


def layer(
    field_hbm, cot_hbm, raw_hbm, skip_in, bias_in,
    d1_ref, d1t_ref, d2_ref, d2t_ref, fwd_ref, inv_ref, eye_ref, order_ref, back_order_ref, repeat_ref,
    out_hbm, sg_hbm, g_hbm, r4, skip_ref, line_ref,
    io_ref, cot_ref, raw_ref, v_ref, ct_ref, out_ref, g_ref, vk_ref, h_ref, b_ref, w_ref,
    x_ref, y_ref, p_ref, kron_ref,
    acc_ref, sum_ref, part_ref, slab_ref, half_ref, dp_ref, total_ref,
    s1, s2, r1, r2, r3,
    send_sem, recv_sem, local_sem, load_sem, store_sem, small_send, small_recv,
):
    dp = lax.axis_index("dp")
    slab = lax.axis_index("slab")
    me = dp * SLAB + slab

    def wait_bytes(ref, sem):
        pltpu.make_async_copy(ref, ref, sem).wait()

    column = [slab] + [lax.rem(slab + step, SLAB) for step in range(1, SLAB)]

    def everybody(act):
        def one(turn, carry):
            for step in range(1, SLAB):
                act(lax.rem(dp + turn + step, DP), column[step])
            return carry

        def own(turn, carry):
            act(lax.rem(dp + turn, DP), slab)
            return carry

        lax.fori_loop(0, DP, one, 0)
        lax.fori_loop(1, DP, own, 0, unroll=True)

    barrier = pltpu.get_barrier_semaphore()
    load_field = pltpu.make_async_copy(field_hbm, io_ref, load_sem.at[0])
    load_raw = pltpu.make_async_copy(raw_hbm, raw_ref, load_sem.at[1])
    load_cot = pltpu.make_async_copy(cot_hbm, cot_ref, load_sem.at[2])
    load_field.start()
    load_raw.start()
    load_cot.start()

    everybody(
        lambda row, place: pl.semaphore_signal(
            barrier, inc=1, device_id=(row, place), device_id_type=MESH
        )
    )

    rest = pl.ds(0, DEVICES - 1)

    def send(s_ref, r_ref, phase, half):
        at = 2 * phase + half
        pltpu.make_async_copy(s_ref.at[half, me], r_ref.at[half, me], local_sem.at[at]).start()

        def one(row, place):
            pltpu.make_async_remote_copy(
                src_ref=s_ref.at[half, row * SLAB + place],
                dst_ref=r_ref.at[half, me],
                send_sem=send_sem.at[at],
                recv_sem=recv_sem.at[at],
                device_id=(row, place),
                device_id_type=MESH,
            ).start()

        everybody(one)

    def arrived(s_ref, r_ref, phase, half):
        at = 2 * phase + half
        pltpu.make_async_copy(s_ref.at[half, me], r_ref.at[half, me], local_sem.at[at]).wait()
        wait_bytes(r_ref.at[half, rest], recv_sem.at[at])

    def sent(s_ref, phase):
        for half in range(2):
            wait_bytes(s_ref.at[half, rest], send_sem.at[2 * phase + half])

    spread_map(skip_in, repeat_ref, kron_ref)
    bias = jnp.concatenate([bias_in[...]] * 4, 1)

    load_field.wait()

    def plane_one(index, carry):
        block = io_ref[:, sixteen(index), :].astype(F32)
        for j in range(2):
            v = rows_apart(block[:, 8 * j : 8 * j + 8]).astype(BF)
            v = dot(order_ref[...], v).astype(BF)
            v_ref[:, columns(2 * index + j)] = v
            store_quad(b_ref, 2 * index + j, dot_nt(d1_ref[...], v))
        return carry

    lax.fori_loop(0, 8, plane_one, 0, unroll=2)
    stage_y(b_ref, d2_ref, s1, 0)
    pl.semaphore_wait(barrier, DEVICES - 1)
    send(s1, r1, 0, 0)
    stage_y(b_ref, d2_ref, s1, 1)
    send(s1, r1, 0, 1)
    load_raw.wait()

    turn_weights(raw_ref, eye_ref, w_ref, 0)
    turn_weights(raw_ref, eye_ref, w_ref, 1)
    for half in range(2):
        arrived(s1, r1, 0, half)
        line_forward(r1, fwd_ref, x_ref, half)
        mix(x_ref, w_ref, p_ref, half)
        line_inverse(p_ref, inv_ref, s2, half)
        send(s2, r2, 1, half)

    load_cot.wait()

    def prepare(index, carry):
        block = cot_ref[:, sixteen(index), :].astype(F32)
        for j in range(2):
            quad = columns(2 * index + j)
            cot = rows_apart(block[:, 8 * j : 8 * j + 8]).astype(BF)
            cot = dot(order_ref[...], cot).astype(BF)
            ct_ref[quad, :] = dot_nt(eye_ref[...], cot).astype(BF)
            vt = dot_nt(eye_ref[...], v_ref[:, quad]).astype(BF)
            vk_ref[quad, :] = dot(vt, kron_ref[...]) + bias
        return carry

    lax.fori_loop(0, 8, prepare, 0, unroll=2)
    for half in range(2):
        arrived(s2, r2, 1, half)
        unstage_y(r2, d2t_ref, h_ref, half)

    def point(index, carry):
        for j in range(2):
            quad = 2 * index + j
            pre = dot(d1t_ref[...], load_quad(h_ref, quad)) + vk_ref[columns(quad), :]
            square = pre * pre
            half = 0.5 + 0.5 * jnp.tanh(pre * (ROOT + (ROOT * 0.044715) * square))
            out = pre * half
            out_ref[columns(quad), :] = out.astype(BF)
            slope = half + out * (1.0 - half) * (2.0 * ROOT + (6.0 * 0.044715 * ROOT) * square)
            g = (ct_ref[columns(quad), :].astype(F32) * slope).astype(BF)
            g_ref[columns(quad), :] = g
            store_quad(b_ref, quad, dot(d1_ref[...], g))
        return carry

    lax.fori_loop(0, 8, point, 0, unroll=4)
    sent(s1, 0)
    for half in range(2):
        stage_y(b_ref, d2_ref, s1, half)
        send(s1, r3, 2, half)

    store_g = pltpu.make_async_copy(g_ref, g_hbm, store_sem.at[2])
    store_g.start()

    acc_ref[...] = jnp.zeros_like(acc_ref)
    sum_ref[...] = jnp.zeros_like(sum_ref)

    def outer(quad, carry):
        g = g_ref[columns(quad), :]
        acc_ref[...] += dot(v_ref[:, columns(quad)], g)
        sum_ref[...] += jnp.sum(g.astype(F32).reshape(32, 8, 256), axis=0)
        return carry

    lax.fori_loop(0, 16, outer, 0, unroll=2)
    acc = acc_ref[...]
    low = low_lanes((64, 128))
    a = acc[:64, :128] + acc[128:192, 128:]
    b = acc[64:128, :128] + acc[192:, 128:]
    part_ref[pl.ds(0, 8)] = jnp.where(low, a + swap(b), 0.0).reshape(8, 8, 128)
    line = jnp.sum(sum_ref[...], axis=0, keepdims=True)
    line = line[:, :128] + line[:, 128:]
    line = line + swap(line)
    part_ref[8] = jnp.broadcast_to(line, (8, 128))
    part_ref[pl.ds(9, 7)] = jnp.zeros((7, 8, 128), F32)

    def along_slab(source, target_ref, at, number):
        for step in range(1, SLAB):
            pltpu.make_async_remote_copy(
                src_ref=source(column[step]),
                dst_ref=target_ref.at[at],
                send_sem=small_send.at[number],
                recv_sem=small_recv.at[number],
                device_id=(dp, column[step]),
                device_id_type=MESH,
            ).start()

    few = pl.ds(0, SLAB - 1)
    along_slab(lambda place: part_ref.at[place], slab_ref, slab, 0)

    def turn_out(index, carry):
        both = []
        for j in range(2):
            both.append(rows_together(dot_nt(back_order_ref[...], out_ref[columns(2 * index + j), :])))
        io_ref[:, sixteen(index), :] = jnp.concatenate(both, 1).astype(BF)
        return carry

    lax.fori_loop(0, 8, turn_out, 0, unroll=2)
    store_out = pltpu.make_async_copy(io_ref, out_hbm, store_sem.at[0])
    store_out.start()

    sent(s2, 1)
    for half in range(2):
        arrived(s1, r3, 2, half)
        line_forward(r3, fwd_ref, y_ref, half)
        mix_back(y_ref, w_ref, p_ref, half)
        line_inverse(p_ref, inv_ref, s2, half)
        send(s2, r4, 3, half)

    wait_bytes(part_ref.at[few], small_send.at[0])
    wait_bytes(slab_ref.at[few], small_recv.at[0])
    slab_ref[slab] = part_ref[slab]
    half_ref[...] = jnp.sum(slab_ref[...], axis=0)

    def along_dp(step, carry):
        pltpu.make_async_remote_copy(
            src_ref=half_ref,
            dst_ref=dp_ref.at[dp],
            send_sem=small_send.at[1],
            recv_sem=small_recv.at[1],
            device_id=(lax.rem(dp + step, DP), slab),
            device_id_type=MESH,
        ).start()
        return carry

    lax.fori_loop(1, DP, along_dp, 0)
    weight_gradient(x_ref, y_ref, eye_ref, raw_ref, w_ref)
    store_sg = pltpu.make_async_copy(raw_ref, sg_hbm, store_sem.at[1])
    store_sg.start()

    seven = pl.ds(0, DP - 1)
    wait_bytes(dp_ref.at[seven], small_send.at[1])
    wait_bytes(dp_ref.at[seven], small_recv.at[1])
    dp_ref[dp] = half_ref[...]
    part_ref[slab] = jnp.sum(dp_ref[...], axis=0) * FACTOR
    total_ref[slab] = part_ref[slab]
    along_slab(lambda place: part_ref.at[slab], total_ref, slab, 2)

    sent(s1, 2)
    sent(s2, 3)
    wait_bytes(part_ref.at[few], small_send.at[2])
    wait_bytes(total_ref.at[few], small_recv.at[2])
    skip_ref[...] = total_ref[pl.ds(0, 8)].reshape(64, 128)[:, :64]
    line_ref[...] = total_ref[8][:1, :64]
    store_out.wait()
    store_sg.wait()
    store_g.wait()
    for half in range(2):
        arrived(s2, r4, 3, half)


def finish(
    skip_in, skip_part, line_part, repeat_ref, r_hbm, g_hbm, d1t_hbm, d2t_hbm, order_hbm, out_part, sg_part,
    back_hbm, skip_ref, line_ref, out_hbm, sg_hbm,
    r_ref, g_ref, d1t_ref, d2t_ref, back_order_ref, out_ref, sg_ref,
    back_ref, h_ref, kron_ref, load_sem, copy_sem, store_sem,
):
    sources = (r_hbm, d2t_hbm, d1t_hbm, order_hbm, g_hbm, out_part, sg_part)
    targets = (r_ref, d2t_ref, d1t_ref, back_order_ref, g_ref, out_ref, sg_ref)
    loads = [
        pltpu.make_async_copy(source, target, load_sem.at[i])
        for i, (source, target) in enumerate(zip(sources, targets))
    ]
    for load in loads[:5]:
        load.start()
    skip_ref[...] = skip_part[...]
    line_ref[...] = line_part[...]
    spread_map(skip_in, repeat_ref, kron_ref)
    loads[0].wait()
    loads[1].wait()
    for half in range(2):
        unstage_y(r_ref, d2t_ref, h_ref, half)
    for load in loads[2:5]:
        load.wait()
    for load in loads[5:]:
        load.start()

    def last(index, carry):
        both = []
        for j in range(2):
            quad = 2 * index + j
            value = dot(d1t_ref[...], load_quad(h_ref, quad)) + dot_nt(
                g_ref[columns(quad), :], kron_ref[...]
            )
            both.append(rows_together(dot_nt(back_order_ref[...], value.astype(BF))))
        back_ref[:, sixteen(index), :] = jnp.concatenate(both, 1).astype(BF)
        return carry

    def store_back(part):
        rows = pl.ds(32 * part, 32)
        return pltpu.make_async_copy(back_ref.at[:, rows], back_hbm.at[:, rows], store_sem.at[part])

    lax.fori_loop(0, 2, last, 0, unroll=2)
    store_back(0).start()
    lax.fori_loop(2, 4, last, 0, unroll=2)
    store_back(1).start()
    moves = [
        pltpu.make_async_copy(out_ref, out_hbm, copy_sem.at[0]),
        pltpu.make_async_copy(sg_ref, sg_hbm, copy_sem.at[1]),
    ]
    for load, move in zip(loads[5:], moves):
        load.wait()
        move.start()
    lax.fori_loop(4, 6, last, 0, unroll=2)
    store_back(2).start()
    lax.fori_loop(6, 8, last, 0, unroll=2)
    store_back(3).start()
    for move in moves:
        move.wait()
    for part in range(4):
        store_back(part).wait()


WHOLE = pl.BlockSpec(memory_space=pltpu.VMEM)
AWAY = pl.BlockSpec(memory_space=pl.ANY)


def shards(field, cotangent, spectral, skip, bias):
    constants = tuple(jnp.asarray(a) for a in tables())
    d1, d1t, d2, d2t, fwd, inv, eye, order, back_order, repeat = constants
    shape = lambda dims, dtype: jax.ShapeDtypeStruct(dims, dtype)

    def gather(a):
        return jnp.transpose(a.reshape(C, 4, 32, 128), (0, 2, 1, 3)).reshape(C, 128, 128)

    def spread(a):
        return jnp.transpose(a.reshape(C, 32, 4, 128), (0, 2, 1, 3)).reshape(1, C, 4, N * N)

    grid = pltpu.VMEM((256, N * N), BF)
    turned = pltpu.VMEM((N * N, 256), BF)
    block = pltpu.VMEM((C, 128, 128), BF)
    planes = pltpu.VMEM((8, 512, 256), BF)
    modes = pltpu.VMEM((2048, 128), F32)
    chunks = pltpu.VMEM((2, DEVICES, 16, 128), BF)
    square = pltpu.VMEM((256, 256), BF)
    small = lambda count: pltpu.VMEM((count, 8, 128), F32)
    dma = pltpu.SemaphoreType.DMA
    narrow = (shape((C, C), F32), shape((1, C), F32))
    weights = shape((2, C, C, 256), BF)
    cells = shape((C, 128, 128), BF)
    out, spectral_grad, g, r4, skip_grad, bias_grad = pl.pallas_call(
        layer,
        out_shape=(
            cells, weights, shape((N * N, 256), BF), shape((2, DEVICES, 16, 128), BF), *narrow
        ),
        in_specs=[AWAY, AWAY, AWAY] + [WHOLE] * 12,
        out_specs=[AWAY] * 4 + [WHOLE] * 2,
        scratch_shapes=[
            block, block, pltpu.VMEM((2, C, C, 256), BF), grid, turned, turned, turned,
            pltpu.VMEM((N * N, 256), F32), planes, planes, pltpu.VMEM((256 * PITCH, 128), F32),
            modes, modes, modes, pltpu.VMEM((256, 256), BF),
            pltpu.VMEM((256, 256), F32), pltpu.VMEM((8, 256), F32),
            small(16), small(16), pltpu.VMEM((8, 128), F32), small(8), small(16),
        ]
        + [chunks] * 5
        + [dma((8,)), dma((8,)), dma((8,)), dma((3,)), dma((3,)), dma((3,)), dma((3,))],
        compiler_params=pltpu.CompilerParams(
            collective_id=1, has_side_effects=True, vmem_limit_bytes=VMEM_LIMIT
        ),
        name="layer",
    )(gather(field), gather(cotangent), spectral, skip, bias.reshape(1, C), *constants)
    back, skip_grad, bias_grad, out, spectral_grad = pl.pallas_call(
        finish,
        out_shape=(cells, *narrow, cells, weights),
        in_specs=[WHOLE] * 4 + [AWAY] * 7,
        out_specs=[AWAY, WHOLE, WHOLE, AWAY, AWAY],
        scratch_shapes=[
            chunks, turned, square, pltpu.VMEM((512, 256), BF), square, block,
            pltpu.VMEM((2, C, C, 256), BF), block, planes, square,
            dma((7,)), dma((2,)), dma((4,)),
        ],
        compiler_params=pltpu.CompilerParams(vmem_limit_bytes=VMEM_LIMIT),
        name="finish",
    )(skip, skip_grad, bias_grad, repeat, r4, g, d1t, d2t, back_order, out, spectral_grad)
    return (spread(out), spread(back), spectral_grad, skip_grad, bias_grad[0])


def solution(mesh):
    whole = P("dp", None, "slab", None)
    modes = P(None, None, None, ("slab", "dp"))
    return jax.shard_map(
        shards,
        mesh=mesh,
        in_specs=(whole, whole, modes, P(), P()),
        out_specs=(whole, whole, modes, P(), P()),
        check_vma=False,
    )
```
